256 devices in a mesh: seq: 64 (over z, x, core), grp: 4 (over y).
Axes of the slice: x: 4, y: 4, z: 8, core: 2. Of those that a mesh axis runs over, the one named last changes fastest.
Arguments:
- queries: bfloat16 [98304, 1024], P(('grp', 'seq')), parts along dimension 0, may hold values from -8 to 8
- keys: bfloat16 [98304, 1024], P(('grp', 'seq')), parts along dimension 0, may hold values from -8 to 8
- values: bfloat16 [98304, 1024], P(('grp', 'seq')), parts along dimension 0, may hold values from -6 to 6
- grad_out: bfloat16 [98304, 1024], P(('grp', 'seq')), parts along dimension 0, may hold values from -6 to 6
- cluster: int32 [8, 98304, 1], P(None, ('grp', 'seq')), parts along dimension 1, may hold values from 0 to 63; in each aligned block of 384 rows (0 to 383, 384 to 767, ..., all dimensions but the last counted through in order) at most 12 rows name the same one
Outputs:
- attn_out: bfloat16 [98304, 1024], P(('grp', 'seq')), parts along dimension 0
- grad_query: bfloat16 [98304, 1024], P(('grp', 'seq')), parts along dimension 0
- grad_key: bfloat16 [98304, 1024], P(('grp', 'seq')), parts along dimension 0
- grad_value: bfloat16 [98304, 1024], P(('grp', 'seq')), parts along dimension 0
The draws below stay inside these ranges and needn't reach their ends.
There are 4 independent parts, one for each index of `grp`. The reference program is written for one: setup_inputs(seed, part) draws one part's arguments, and reference() takes and returns one part's arrays. A program takes and returns all parts, laid end to end along the dimension named above; each array names one. Nothing has to cross between parts.
Inputs may be any that keep to these rules, and one draw needn't show every extreme that they name: In each head, the 384 tokens of one device name one cluster at most 12 times.
All inputs are finite; a program needn't handle non-finite values.
Results may differ from the reference program's by a relative error of at most 0.017.
The reference program's roundings to bfloat16 on the way count: a program that leaves them out, or rounds other values in their place, can miss the bound.
Values may be sent and summed in bfloat16 or wider, within the bound.
A program may use at most 64 MiB of HBM per device.

```python
import math
import jax
import jax.numpy as jnp
import numpy as np
from jax import lax

HEADS = 8
HEAD_DIM = 128
TOK_DEV = 384
TOKENS = 24576
CLUSTERS = 64
MOST = 12
CAP = 768


def draw_queries(key, part):
    key = jax.random.fold_in(key, 1)
    second_key = jax.random.fold_in(key, 1)
    jitter = jax.random.truncated_normal(second_key, -4.0, 4.0, (TOKENS, HEADS * HEAD_DIM), jnp.float32)
    result = jitter
    return result.astype(jnp.bfloat16)


def draw_keys(key, part):
    key = jax.random.fold_in(key, 2)
    second_key = jax.random.fold_in(key, 1)
    jitter = jax.random.truncated_normal(second_key, -4.0, 4.0, (TOKENS, HEADS * HEAD_DIM), jnp.float32)
    result = jitter
    return result.astype(jnp.bfloat16)


def levels(own_key, extent, cuts, least, top_value):
    level, own = 1.0, jax.random.fold_in(own_key, 6)
    for position, parts in cuts:
        steps = jnp.exp(jax.random.uniform(jax.random.fold_in(own, position), (parts,), jnp.float32, least / len(cuts), top_value / len(cuts)))
        level = level * jnp.repeat(steps, extent[position] // parts).reshape([-1 if axis == position else 1 for axis in range(len(extent))])
    return level


def assign_block(rng, own, number, rows, amount, top, most, lean):
    order = jax.random.permutation(rng, amount)
    crowded, common = load_shares(amount, rows * top, most, lean, True), load_shares(amount, rows * top, most, lean, False)
    places = jnp.arange(amount)

    def named(lengths, rotation):
        used = int((lengths > 0).sum())
        fixed = max(1, used // 4)
        passed = fixed + (places - fixed + rotation * (used - fixed)) % max(1, amount - fixed)
        return jnp.zeros((amount,), jnp.int32).at[order[jnp.where(places < fixed, places, passed)]].set(jnp.asarray(lengths, jnp.int32))

    lengths = jnp.where(number % 4 == 0, named(crowded, number // 4), named(common, number - number // 4 - 1))
    mixed = jax.random.permutation(jax.random.fold_in(own, 3), amount)
    donor, sink = mixed[0:amount // 2 * 2:2], mixed[1:amount // 2 * 2:2]
    margin = jnp.minimum(lengths[donor] - 1, most - lengths[sink]) // 2
    margin = jnp.where((donor == order[0]) | (sink == order[0]) | (lengths[sink] == 0), 0, jnp.maximum(margin, 0))
    passed = jax.random.randint(jax.random.fold_in(own, 4), (amount // 2,), 0, 1 << 20) % (margin + 1)
    lengths = lengths.at[donor].add(-passed).at[sink].add(passed)
    members = jnp.searchsorted(jnp.cumsum(lengths), jnp.arange(rows * top), side="right").astype(jnp.int32)
    listing = members.reshape(top, rows).T
    listing = listing[jax.random.permutation(jax.random.fold_in(own, 1), rows)]
    rotation = jax.random.randint(jax.random.fold_in(own, 2), (rows, 1), 0, top)
    return jnp.take_along_axis(listing, (jnp.arange(top)[None, :] + rotation) % top, axis=1)


def load_shares(count, total, most, slope, full):
    portions = [(1 << 20) // math.isqrt(rank ** slope) + 1 for rank in range(1, count + 1)]
    largest = most if full else min(most, max(-(-total // count), total * portions[0] // sum(portions)))
    least = 1 if total - largest >= count - 1 else 0
    given, surplus = [largest] + [least] * (count - 1), total - largest - least * (count - 1)
    while surplus > 0:
        candidates = [i for i in range(1, count) if given[i] < largest] or [i for i in range(1, count) if given[i] < most]
        whole, remaining = sum([portions[i] for i in candidates]), surplus
        for i in candidates:
            addition = min(most - given[i], max(1, remaining * portions[i] // whole), surplus)
            given[i] = given[i] + addition
            surplus = surplus - addition
    return np.array(given)


def bell_draw(key, shape, scale, limit, shards=(), held_as=jnp.bfloat16):
    entries = jax.random.normal(key, shape, jnp.float32) * scale
    if len(shards) > 0:
        entries = levels(key, shape, shards, -0.22, 0.18) * entries
    return jnp.clip(entries, min=-limit, max=limit).astype(held_as)


def setup_inputs(seed: int = 0, part: int = 0) -> dict:
    seeds = jax.random.split(jax.random.key(seed), 6)
    part_splits = jax.random.split(jax.random.fold_in(seeds[5], part), 6)
    queries = draw_queries(jax.random.fold_in(jax.random.fold_in(seeds[5], part), 71), part)
    keys = draw_keys(jax.random.fold_in(jax.random.fold_in(seeds[5], part), 71), part)
    values = bell_draw(part_splits[2], (TOKENS, HEADS * HEAD_DIM), 1.0, 6.0, ((0, 64),))
    grad_out = bell_draw(part_splits[3], (TOKENS, HEADS * HEAD_DIM), 1.0, 6.0, ((0, 64),))
    cluster_keys = jax.random.split(jax.random.fold_in(part_splits[4], 1), HEADS * TOKENS // TOK_DEV)
    cluster_turns = jax.random.permutation(jax.random.fold_in(part_splits[4], 3), HEADS * TOKENS // TOK_DEV)
    cluster = jax.vmap(lambda own, number: assign_block(jax.random.fold_in(part_splits[4], 2), own, number, TOK_DEV, CLUSTERS, 1, MOST, 2))(cluster_keys, cluster_turns).reshape((HEADS, TOKENS, 1))
    return dict(queries=queries, keys=keys, values=values, grad_out=grad_out, cluster=cluster)


def probabilities(query_slots, key_slots, valid_mask, score_scale):
    scores = jnp.einsum('...id,...jd->...ij', query_slots, key_slots) * score_scale
    ladder = jnp.arange(scores.shape[-1])
    allowed = valid_mask[..., :, None] & valid_mask[..., None, :] & (ladder[None, :] <= ladder[:, None])
    scores = jnp.where(allowed, scores, -1e30)
    largest = jnp.max(scores, axis=-1, keepdims=True)
    powered = jnp.exp(scores - largest)
    return powered / jnp.sum(powered, axis=-1, keepdims=True)


def to_bf16_and_back(array):
    return lax.optimization_barrier(array.astype(jnp.bfloat16)).astype(jnp.float32)


def head_pass(packed):
    query_head, key_head, value_head, grad_head, labels = packed
    token_count = query_head.shape[0]
    score_scale = HEAD_DIM ** -0.5
    positions = jnp.arange(token_count, dtype=jnp.int32)
    sorted_order = jnp.argsort(labels, stable=True).astype(jnp.int32)
    counts = jax.ops.segment_sum(jnp.ones_like(labels), labels, num_segments=CLUSTERS)
    starts = (jnp.cumsum(counts) - counts).astype(jnp.int32)
    ranking = jnp.zeros((token_count,), jnp.int32).at[sorted_order].set(positions - starts[labels[sorted_order]])
    slot_table = jnp.full((CLUSTERS, CAP), token_count, jnp.int32).at[labels, ranking].set(positions)
    valid_mask = slot_table < token_count
    safe_index = jnp.minimum(slot_table, token_count - 1)

    def gather_slots(source):
        return jnp.where(valid_mask[..., None], source[safe_index].astype(jnp.float32), 0.0)

    query_slots = gather_slots(query_head)
    key_slots = gather_slots(key_head)
    value_slots = gather_slots(value_head)
    grad_slots = gather_slots(grad_head)
    weights = probabilities(query_slots, key_slots, valid_mask, score_scale)
    rounded = to_bf16_and_back(weights)
    output_slots = jnp.einsum('...ij,...jd->...id', rounded, value_slots)
    output_rounded = to_bf16_and_back(output_slots)
    grad_value = jnp.einsum('...ij,...id->...jd', rounded, grad_slots)
    grad_weights = jnp.einsum('...id,...jd->...ij', grad_slots, value_slots)
    row_dot = jnp.sum(grad_slots * output_rounded, axis=-1, keepdims=True)
    score_grad = to_bf16_and_back(weights * (grad_weights - row_dot))
    grad_query = jnp.einsum('...ij,...jd->...id', score_grad, key_slots) * score_scale
    grad_key = jnp.einsum('...ij,...id->...jd', score_grad, query_slots) * score_scale

    def token_rows(result):
        return result[labels, ranking].astype(jnp.bfloat16)

    return token_rows(output_slots), token_rows(grad_query), token_rows(grad_key), token_rows(grad_value)


def reference(queries, keys, values, grad_out, cluster):
    token_count = queries.shape[0]

    def split_heads(array):
        return array.reshape(token_count, HEADS, HEAD_DIM).transpose(1, 0, 2)

    def merge_heads(array):
        return array.transpose(1, 0, 2).reshape(token_count, HEADS * HEAD_DIM)

    results = lax.map(head_pass, (split_heads(queries), split_heads(keys), split_heads(values), split_heads(grad_out), cluster[:, :, 0]))
    return merge_heads(results[0]), merge_heads(results[1]), merge_heads(results[2]), merge_heads(results[3])
```

```python
import functools

import jax
import jax.numpy as jnp
import numpy as np
from jax import lax
from jax.experimental import pallas as pl
from jax.experimental.pallas import tpu as pltpu
from jax.sharding import PartitionSpec as P

MESH = pl.DeviceIdType.MESH
HEADS = 8
DIM = 128
ROWS = 384
CLUSTERS = 64
MOST = 12
LINE = 8
OWNED = 8
PIECE = OWNED * MOST
SLOTS = LINE * PIECE
CAP = LINE * LINE * MOST
HALF = SLOTS // 2
ABSENT = 64.0
NEG = -1e30
VMEM = pltpu.VMEM
ANY = pl.ANY


def place(i):
    return jnp.where(i % 2 == 1, (i + 1) // 2, (LINE - i // 2) % LINE)


def greet(z, r):
    barrier = pltpu.get_barrier_semaphore()
    for i in range(1, LINE):
        pl.semaphore_signal(
            barrier, inc=1, device_id={"seq": lax.rem(z + i, LINE) * LINE + r}, device_id_type=MESH
        )
        pl.semaphore_signal(
            barrier, inc=1, device_id={"seq": z * LINE + lax.rem(r + i, LINE)}, device_id_type=MESH
        )
    pl.semaphore_wait(barrier, 2 * (LINE - 1))


def wait_for(ref, sem):
    pltpu.make_async_copy(ref, ref, sem).wait()


def piece(o):
    return pl.ds(pl.multiple_of(o * PIECE, PIECE), PIECE)


def lanes(h):
    return pl.ds(pl.multiple_of(h * DIM, DIM), DIM)


def gather_kernel(
    q_ref, k_ref, v_ref, g_ref, label_ref, order_ref,
    out_ref, slot_ref,
    zbuf, zlab, xsrc, xbuf, z_send, z_recv, l_send, l_recv, x_send, x_recv,
):
    me = lax.axis_index("seq")
    z, r = me // LINE, me % LINE
    sources = (q_ref, k_ref, v_ref, g_ref)
    greet(z, r)

    def send_z(i, _):
        to = (z + place(i)) % LINE
        peer = {"seq": to * LINE + r}
        pltpu.make_async_remote_copy(
            src_ref=label_ref.at[to], dst_ref=zlab.at[z], send_sem=l_send, recv_sem=l_recv.at[z],
            device_id=peer, device_id_type=MESH,
        ).start()
        for a in range(4):
            pltpu.make_async_remote_copy(
                src_ref=sources[a].at[:, lanes(to)], dst_ref=zbuf.at[z, a],
                send_sem=z_send.at[i], recv_sem=z_recv.at[z],
                device_id=peer, device_id_type=MESH,
            ).start()
        return 0

    pltpu.make_async_copy(label_ref.at[z], zlab.at[z], l_recv.at[z]).start()
    for a in range(4):
        pltpu.make_async_copy(
            sources[a].at[:, lanes(z)], zbuf.at[z, a], z_recv.at[z]
        ).start()
    lax.fori_loop(1, LINE, send_z, 0)

    before = (
        lax.broadcasted_iota(jnp.int32, (ROWS, ROWS), 0)
        < lax.broadcasted_iota(jnp.int32, (ROWS, ROWS), 1)
    ).astype(jnp.float32).astype(jnp.bfloat16)

    def regroup(s):
        wait_for(xbuf.at[s], x_recv.at[s])
        for half in range(2):
            moved = jnp.dot(
                order_ref[...], xbuf[s, half * HALF:(half + 1) * HALF],
                preferred_element_type=jnp.float32,
            ).astype(jnp.bfloat16)
            for j in range(OWNED):
                at = pl.multiple_of(s * PIECE + half * 48, 16)
                out_ref[j, pl.ds(at, 48), :] = moved[j * 48:(j + 1) * 48]

    def step(i, _):
        s = (z - place(i) + LINE) % LINE
        wait_for(zlab.at[s], l_recv.at[s])
        label = zlab[s]
        named = (
            lax.broadcasted_iota(jnp.int32, (CLUSTERS, ROWS), 0) == label
        ).astype(jnp.float32)
        earlier = jnp.dot(
            named.astype(jnp.bfloat16), before, preferred_element_type=jnp.float32
        )
        rank = jnp.sum(named * earlier, axis=0, keepdims=True)
        slot = label * MOST + rank.astype(jnp.int32)
        slot_ref[s] = slot
        pick = (
            lax.broadcasted_iota(jnp.int32, (SLOTS, ROWS), 0) == slot
        ).astype(jnp.float32)
        used = jnp.sum(pick, axis=1, keepdims=True)
        mark = jnp.where(
            lax.broadcasted_iota(jnp.int32, (SLOTS, DIM), 1) == 0, (1.0 - used) * ABSENT, 0.0
        )
        pick = pick.astype(jnp.bfloat16)
        wait_for(zbuf.at[s], z_recv.at[s])
        for a in range(4):
            packed = jnp.dot(pick, zbuf[s, a], preferred_element_type=jnp.float32)
            if a == 1:
                packed = packed + mark
            xsrc[s, :, a * DIM:(a + 1) * DIM] = packed.astype(jnp.bfloat16)
        pltpu.make_async_copy(xsrc.at[s, piece(r)], xbuf.at[s, piece(r)], x_recv.at[s]).start()

        def send_x(n, _):
            o = (r + n) % LINE
            pltpu.make_async_remote_copy(
                src_ref=xsrc.at[s, piece(o)], dst_ref=xbuf.at[s, piece(r)],
                send_sem=x_send.at[s], recv_sem=x_recv.at[s],
                device_id={"seq": z * LINE + o}, device_id_type=MESH,
            ).start()
            return 0

        lax.fori_loop(1, LINE, send_x, 0)

        @pl.when(i > 0)
        def _():
            regroup((z - place(i - 1) + LINE) % LINE)

        return 0

    lax.fori_loop(0, LINE, step, 0)
    regroup((z - place(LINE - 1) + LINE) % LINE)

    def drain(i, _):
        wait_for(xsrc.at[i, pl.ds(0, SLOTS - PIECE)], x_send.at[i])

        @pl.when(i > 0)
        def _():
            wait_for(zbuf.at[i], z_send.at[i])
            wait_for(zlab.at[i], l_send)

        return 0

    lax.fori_loop(0, LINE, drain, 0)


def attend_kernel(x_ref, out_ref, dk_acc, dv_acc):
    scale = DIM ** -0.5
    block = 256
    k_all = x_ref[0, :, DIM:2 * DIM]
    v_all = x_ref[0, :, 2 * DIM:3 * DIM]
    first = (lax.broadcasted_iota(jnp.int32, (8, DIM), 1) == 0).astype(jnp.float32).astype(jnp.bfloat16)
    marks = lax.dot_general(
        first, k_all, (((1,), (1,)), ((), ())), preferred_element_type=jnp.float32
    )[0:1]
    bias = jnp.where(marks > ABSENT / 2, NEG, 0.0)
    for b in range(CAP // block):
        lo, hi = b * block, (b + 1) * block
        q = x_ref[0, lo:hi, 0:DIM]
        g = x_ref[0, lo:hi, 3 * DIM:4 * DIM]
        k, v = k_all[:hi], v_all[:hi]
        scores = lax.dot_general(
            q, k, (((1,), (1,)), ((), ())), preferred_element_type=jnp.float32
        ) * scale
        scores = scores + bias[:, :hi]
        late = (
            lax.broadcasted_iota(jnp.int32, (block, hi), 1)
            > lax.broadcasted_iota(jnp.int32, (block, hi), 0) + lo
        )
        scores = jnp.where(late, NEG, scores)
        powered = jnp.exp(scores - jnp.max(scores, axis=-1, keepdims=True))
        weights = powered * (1.0 / jnp.sum(powered, axis=-1, keepdims=True))
        rounded = weights.astype(jnp.bfloat16)
        o = jnp.dot(rounded, v, preferred_element_type=jnp.float32).astype(jnp.bfloat16)
        out_ref[0, lo:hi, 0:DIM] = o
        dv = lax.dot_general(
            rounded, g, (((0,), (0,)), ((), ())), preferred_element_type=jnp.float32
        )
        grad_weights = lax.dot_general(
            g, v, (((1,), (1,)), ((), ())), preferred_element_type=jnp.float32
        )
        row_dot = jnp.sum(
            g.astype(jnp.float32) * o.astype(jnp.float32), axis=-1, keepdims=True
        )
        ds = (weights * (grad_weights - row_dot)).astype(jnp.bfloat16)
        dq = jnp.dot(ds, k, preferred_element_type=jnp.float32) * scale
        out_ref[0, lo:hi, DIM:2 * DIM] = dq.astype(jnp.bfloat16)
        dk = lax.dot_general(
            ds, q, (((0,), (0,)), ((), ())), preferred_element_type=jnp.float32
        )
        if b == 0:
            dk_acc[lo:hi], dv_acc[lo:hi] = dk, dv
        else:
            dk_acc[:lo] += dk[:lo]
            dv_acc[:lo] += dv[:lo]
            dk_acc[lo:hi], dv_acc[lo:hi] = dk[lo:], dv[lo:]
    out_ref[0, :, 2 * DIM:3 * DIM] = (dk_acc[...] * scale).astype(jnp.bfloat16)
    out_ref[0, :, 3 * DIM:4 * DIM] = dv_acc[...].astype(jnp.bfloat16)


def return_kernel(
    y_ref, slot_ref, order_ref,
    o_ref, dq_ref, dk_ref, dv_ref,
    xsrc, xbuf, zsrc, x_send, x_recv, z_send, z_recv,
):
    me = lax.axis_index("seq")
    z, r = me // LINE, me % LINE
    results = (o_ref, dq_ref, dk_ref, dv_ref)
    greet(z, r)

    def spread(i):
        s = (z + place(i)) % LINE
        for half in range(2):
            at = pl.multiple_of(s * PIECE + half * 48, 16)
            taken = jnp.concatenate([y_ref[j, pl.ds(at, 48), :] for j in range(OWNED)], axis=0)
            xsrc[s, half * HALF:(half + 1) * HALF] = jnp.dot(
                order_ref[...], taken, preferred_element_type=jnp.float32
            ).astype(jnp.bfloat16)
        pltpu.make_async_copy(xsrc.at[s, piece(r)], xbuf.at[s, piece(r)], x_recv.at[s]).start()

        def send_x(n, _):
            o = (r + n) % LINE
            pltpu.make_async_remote_copy(
                src_ref=xsrc.at[s, piece(o)], dst_ref=xbuf.at[s, piece(r)],
                send_sem=x_send.at[s], recv_sem=x_recv.at[s],
                device_id={"seq": z * LINE + o}, device_id_type=MESH,
            ).start()
            return 0

        lax.fori_loop(1, LINE, send_x, 0)

    def deliver(i, own):
        s = (z + place(i)) % LINE
        wide = jnp.broadcast_to(slot_ref[s].astype(jnp.float32), (DIM, ROWS))
        column = wide.T[:, 0:1].astype(jnp.int32)
        pick = (
            lax.broadcasted_iota(jnp.int32, (ROWS, SLOTS), 1) == column
        ).astype(jnp.float32).astype(jnp.bfloat16)
        wait_for(xbuf.at[s], x_recv.at[s])
        for a in range(4):
            zsrc[s, a] = jnp.dot(
                pick, xbuf[s, :, a * DIM:(a + 1) * DIM], preferred_element_type=jnp.float32
            ).astype(jnp.bfloat16)
        for a in range(4):
            if own:
                pltpu.make_async_copy(
                    zsrc.at[s, a], results[a].at[:, lanes(z)], z_recv.at[z]
                ).start()
            else:
                pltpu.make_async_remote_copy(
                    src_ref=zsrc.at[s, a], dst_ref=results[a].at[:, lanes(z)],
                    send_sem=z_send.at[s], recv_sem=z_recv.at[z],
                    device_id={"seq": s * LINE + r}, device_id_type=MESH,
                ).start()

    spread(0)
    spread(1)
    deliver(0, True)

    def step(i, _):
        spread(i + 1)
        deliver(i, False)
        return 0

    lax.fori_loop(1, LINE - 1, step, 0)
    deliver(LINE - 1, False)

    def drain(i, _):
        wait_for(xsrc.at[i, pl.ds(0, SLOTS - PIECE)], x_send.at[i])
        wait_for(zsrc.at[i], z_recv.at[i])

        @pl.when(i != z)
        def _():
            wait_for(zsrc.at[i], z_send.at[i])

        return 0

    lax.fori_loop(0, LINE, drain, 0)


def regroup_order():
    out = np.arange(HALF)
    source = (out % 48) // MOST * PIECE + out // 48 * MOST + out % MOST
    return (np.arange(HALF)[None, :] == source[:, None]).astype(np.float32)


def per_device(queries, keys, values, grad_out, cluster):
    dma = pltpu.SemaphoreType.DMA
    bf16 = jnp.bfloat16
    labels = cluster.reshape(HEADS, 1, ROWS)
    order = jnp.asarray(regroup_order(), bf16)
    slots, numbers = pl.pallas_call(
        gather_kernel,
        out_shape=(
            jax.ShapeDtypeStruct((OWNED, CAP, 4 * DIM), bf16),
            jax.ShapeDtypeStruct((LINE, 1, ROWS), jnp.int32),
        ),
        in_specs=[pl.BlockSpec(memory_space=ANY)] * 4 + [pl.BlockSpec(memory_space=VMEM)] * 2,
        out_specs=[pl.BlockSpec(memory_space=VMEM)] * 2,
        scratch_shapes=[
            VMEM((LINE, 4, ROWS, DIM), bf16),
            VMEM((LINE, 1, ROWS), jnp.int32),
            VMEM((LINE, SLOTS, 4 * DIM), bf16),
            VMEM((LINE, SLOTS, 4 * DIM), bf16),
            dma((LINE,)), dma((LINE,)), dma, dma((LINE,)), dma((LINE,)), dma((LINE,)),
        ],
        compiler_params=pltpu.CompilerParams(
            collective_id=0, has_side_effects=True, vmem_limit_bytes=56 * 2**20
        ),
        name="gather",
    )(queries, keys, values, grad_out, labels, order)
    results = pl.pallas_call(
        attend_kernel,
        grid=(OWNED,),
        out_shape=jax.ShapeDtypeStruct((OWNED, CAP, 4 * DIM), bf16),
        in_specs=[pl.BlockSpec((1, CAP, 4 * DIM), lambda j: (j, 0, 0))],
        out_specs=pl.BlockSpec((1, CAP, 4 * DIM), lambda j: (j, 0, 0)),
        scratch_shapes=[VMEM((CAP, DIM), jnp.float32), VMEM((CAP, DIM), jnp.float32)],
        compiler_params=pltpu.CompilerParams(vmem_limit_bytes=48 * 2**20),
        name="attend",
    )(slots)
    return pl.pallas_call(
        return_kernel,
        out_shape=[jax.ShapeDtypeStruct((ROWS, HEADS * DIM), bf16)] * 4,
        in_specs=[pl.BlockSpec(memory_space=VMEM)] * 3,
        out_specs=[pl.BlockSpec(memory_space=ANY)] * 4,
        scratch_shapes=[
            VMEM((LINE, SLOTS, 4 * DIM), bf16),
            VMEM((LINE, SLOTS, 4 * DIM), bf16),
            VMEM((LINE, 4, ROWS, DIM), bf16),
            dma((LINE,)), dma((LINE,)), dma((LINE,)), dma((LINE,)),
        ],
        compiler_params=pltpu.CompilerParams(
            collective_id=1, has_side_effects=True, vmem_limit_bytes=56 * 2**20
        ),
        name="return",
    )(results, numbers, order.T)


def solution(mesh):
    return jax.shard_map(
        per_device,
        mesh=mesh,
        in_specs=(
            P(("grp", "seq"), None),
            P(("grp", "seq"), None),
            P(("grp", "seq"), None),
            P(("grp", "seq"), None),
            P(None, ("grp", "seq"), None),
        ),
        out_specs=(P(("grp", "seq"), None),) * 4,
        check_vma=False,
    )
```

```python
import jax
import jax.numpy as jnp
import numpy as np
from jax import lax
from jax.experimental import pallas as pl
from jax.experimental.pallas import tpu as pltpu
from jax.sharding import PartitionSpec as P

MESH = pl.DeviceIdType.MESH
HEADS = 8
DIM = 128
ROWS = 384
CLUSTERS = 64
MOST = 12
LINE = 8
OWNED = 8
PIECE = OWNED * MOST
SLOTS = LINE * PIECE
CAP = LINE * LINE * MOST
HALF = SLOTS // 2
RUN = HALF // OWNED
WINDOW = 4
AHEAD = 2
ABSENT = 64.0
NEG = -1e30
SCALE = DIM ** -0.5
LOG2E = 1.4426950408889634
BLOCK_FWD = 384
BLOCK_BWD = 256
F32, BF16 = jnp.float32, jnp.bfloat16
NT = (((1,), (1,)), ((), ()))
VMEM = pltpu.VMEM
ANY = pl.ANY


def near(i):
    return jnp.where(i % 2 == 1, (i + 1) // 2, (LINE - i // 2) % LINE)


def far(i):
    return jnp.where(i % 2 == 1, 4 - (i + 1) // 2, 4 + i // 2)


def greet(z, r):
    barrier = pltpu.get_barrier_semaphore()
    for i in range(1, LINE):
        pl.semaphore_signal(
            barrier, inc=1, device_id={"seq": lax.rem(z + i, LINE) * LINE + r}, device_id_type=MESH
        )
        pl.semaphore_signal(
            barrier, inc=1, device_id={"seq": z * LINE + lax.rem(r + i, LINE)}, device_id_type=MESH
        )
    pl.semaphore_wait(barrier, 2 * (LINE - 1))


def wait_for(ref, sem):
    pltpu.make_async_copy(ref, ref, sem).wait()


def piece(o):
    return pl.ds(pl.multiple_of(o * PIECE, PIECE), PIECE)


def lanes(h):
    return pl.ds(pl.multiple_of(h * DIM, DIM), DIM)


def dot(a, b):
    return jnp.dot(a, b, preferred_element_type=F32)


def dot_nt(a, b):
    return lax.dot_general(a, b, NT, preferred_element_type=F32)


def mask(m):
    return m.astype(F32).astype(BF16)


def scores(k, q, bias, lo, hi):
    t = dot_nt(k[:hi], q) * (SCALE * LOG2E) + bias[:hi]
    late = (
        lax.broadcasted_iota(jnp.int32, (hi - lo, hi - lo), 0)
        > lax.broadcasted_iota(jnp.int32, (hi - lo, hi - lo), 1)
    )
    own = jnp.where(late, NEG, t[lo:hi])
    return jnp.concatenate([t[:lo], own], axis=0) if lo else own


def forward(x, o_ref, top_ref, inv_ref, j):
    k, vt = x[j, 1], x[j, 2].T
    bias = jnp.where(k[:, 0:1].astype(F32) > ABSENT / 2, NEG, 0.0)
    for lo in range(0, CAP, BLOCK_FWD):
        hi = lo + BLOCK_FWD
        t = scores(k, x[j, 0, lo:hi], bias, lo, hi)
        top = jnp.max(t, axis=0, keepdims=True)
        powered = jnp.exp2(t - top)
        inv = 1.0 / jnp.sum(powered, axis=0, keepdims=True)
        top_ref[j, :, lo:hi] = top
        inv_ref[j, :, lo:hi] = inv
        o_ref[j, lo:hi] = dot(vt[:, :hi], (powered * inv).astype(BF16)).T.astype(BF16)


def backward(x, o_ref, top_ref, inv_ref, dk_acc, dv_acc, j):
    k, v = x[j, 1], x[j, 2]
    kt = k.T
    bias = jnp.where(k[:, 0:1].astype(F32) > ABSENT / 2, NEG, 0.0)
    for lo in range(0, CAP, BLOCK_BWD):
        hi = lo + BLOCK_BWD
        q, g = x[j, 0, lo:hi], x[j, 3, lo:hi]
        t = scores(k, q, bias, lo, hi)
        weights = jnp.exp2(t - top_ref[j, :, lo:hi]) * inv_ref[j, :, lo:hi]
        dv = dot(weights.astype(BF16), g)
        row_dot = jnp.sum(
            (g.astype(F32) * o_ref[j, lo:hi].astype(F32)).T, axis=0, keepdims=True
        )
        ds = (weights * (dot_nt(v[:hi], g) - row_dot)).astype(BF16)
        dk = dot(ds, q)
        x[j, 0, lo:hi] = (dot(kt[:, :hi], ds) * SCALE).T.astype(BF16)
        if lo:
            dk_acc[:lo] += dk[:lo]
            dv_acc[:lo] += dv[:lo]
        dk_acc[lo:hi] = dk[lo:]
        dv_acc[lo:hi] = dv[lo:]
    x[j, 1] = (dk_acc[...] * SCALE).astype(BF16)
    x[j, 2] = dv_acc[...].astype(BF16)


def kernel(
    q_ref, k_ref, v_ref, g_ref, label_ref, order_ref, undo_ref,
    o_ref, dq_ref, dk_ref, dv_ref,
    zbuf, zlab, pick, back, xsrc, xbuf, ybuf, x, out, top, inv, dk_acc, dv_acc,
    z_send, z_recv, l_send, l_recv, x_send, x_recv, y_send, y_recv, o_send, o_recv,
):
    me = lax.axis_index("seq")
    z, r = me // LINE, me % LINE
    sources = (q_ref, k_ref, v_ref, g_ref)
    results = (o_ref, dq_ref, dk_ref, dv_ref)
    greet(z, r)

    def send_z(i, arrays):
        to = (z + near(i)) % LINE
        for a in arrays:
            pltpu.make_async_remote_copy(
                src_ref=sources[a].at[:, lanes(to)], dst_ref=zbuf.at[z, a],
                send_sem=z_send.at[i], recv_sem=z_recv.at[z, a],
                device_id={"seq": to * LINE + r}, device_id_type=MESH,
            ).start()

    def send_label(i, _):
        to = (z + near(i)) % LINE
        pltpu.make_async_remote_copy(
            src_ref=label_ref.at[to], dst_ref=zlab.at[z], send_sem=l_send, recv_sem=l_recv.at[z],
            device_id={"seq": to * LINE + r}, device_id_type=MESH,
        ).start()
        return 0

    def send_unit(u):
        @pl.when(u < LINE)
        def _():
            send_z(u, (0, 1, 2))

        @pl.when((u > LINE) & (u < 2 * LINE))
        def _():
            send_z(u - LINE, (3,))

    pltpu.make_async_copy(label_ref.at[z], zlab.at[z], l_recv.at[z]).start()
    for a in range(4):
        pltpu.make_async_copy(
            sources[a].at[:, lanes(z)], zbuf.at[z, a], z_recv.at[z, a]
        ).start()
    lax.fori_loop(1, LINE, send_label, 0)

    def first(u, _):
        send_z(u, (0, 1, 2))
        return 0

    lax.fori_loop(1, WINDOW, first, 0)

    before = mask(
        lax.broadcasted_iota(jnp.int32, (ROWS, ROWS), 0)
        < lax.broadcasted_iota(jnp.int32, (ROWS, ROWS), 1)
    )

    def to_owners(s, a, buf, send_sem, recv_sem):
        pltpu.make_async_copy(
            xsrc.at[s, a, piece(r)], buf.at[s, a, piece(r)], recv_sem.at[s, a]
        ).start()

        def send(n, _):
            o = (r + n) % LINE
            pltpu.make_async_remote_copy(
                src_ref=xsrc.at[s, a, piece(o)], dst_ref=buf.at[s, a, piece(r)],
                send_sem=send_sem.at[s, a], recv_sem=recv_sem.at[s, a],
                device_id={"seq": z * LINE + o}, device_id_type=MESH,
            ).start()
            return 0

        lax.fori_loop(1, LINE, send, 0)

    def pack(s, a, mark=None):
        wait_for(zbuf.at[s, a], z_recv.at[s, a])
        packed = dot(pick[s], zbuf[s, a])
        if mark is not None:
            packed = packed + mark
        xsrc[s, a] = packed.astype(BF16)
        to_owners(s, a, xbuf, x_send, x_recv)

    def regroup(i, arrays):
        s = (z - near(i) + LINE) % LINE
        for a in arrays:
            wait_for(xbuf.at[s, a], x_recv.at[s, a])
            for half in range(2):
                moved = dot(
                    order_ref[...], xbuf[s, a, half * HALF:(half + 1) * HALF]
                ).astype(BF16)
                for j in range(OWNED):
                    at = pl.multiple_of(s * PIECE + half * RUN, 16)
                    x[j, a, pl.ds(at, RUN), :] = moved[j * RUN:(j + 1) * RUN]

    def arrive(i, _):
        s = (z - near(i) + LINE) % LINE
        wait_for(zlab.at[s], l_recv.at[s])
        label = zlab[s]
        named = (
            lax.broadcasted_iota(jnp.int32, (CLUSTERS, ROWS), 0) == label
        ).astype(F32)
        rank = jnp.sum(named * dot(named.astype(BF16), before), axis=0, keepdims=True)
        slot = label * MOST + rank.astype(jnp.int32)
        chosen = (lax.broadcasted_iota(jnp.int32, (SLOTS, ROWS), 0) == slot).astype(F32)
        used = jnp.sum(chosen, axis=1, keepdims=True)
        mark = jnp.where(
            lax.broadcasted_iota(jnp.int32, (SLOTS, DIM), 1) == 0, (1.0 - used) * ABSENT, 0.0
        )
        pick[s] = chosen.astype(BF16)
        pack(s, 0)
        pack(s, 1, mark)
        pack(s, 2)
        send_unit(i + WINDOW)
        column = jnp.broadcast_to(slot.astype(F32), (DIM, ROWS)).T[:, 0:1].astype(jnp.int32)
        back[s] = mask(lax.broadcasted_iota(jnp.int32, (ROWS, SLOTS), 1) == column)

        @pl.when(i > 0)
        def _():
            regroup(i - 1, (0, 1, 2))

        return 0

    lax.fori_loop(0, LINE, arrive, 0)
    regroup(LINE - 1, (0, 1, 2))

    def arrive_g(i):
        pack((z - near(i) + LINE) % LINE, 3)
        send_unit(i + LINE + WINDOW)

        @pl.when(i > 0)
        def _():
            regroup(i - 1, (3,))

    def spread(i, a):
        s = (z + far(i)) % LINE
        wait_for(xsrc.at[s, a, pl.ds(0, SLOTS - PIECE)], x_send.at[s, a])
        for half in range(2):
            at = pl.multiple_of(s * PIECE + half * RUN, 16)
            taken = jnp.concatenate(
                [
                    out[j, pl.ds(at, RUN), :] if a == 0 else x[j, a - 1, pl.ds(at, RUN), :]
                    for j in range(OWNED)
                ],
                axis=0,
            )
            xsrc[s, a, half * HALF:(half + 1) * HALF] = dot(undo_ref[...], taken).astype(BF16)
        to_owners(s, a, ybuf, y_send, y_recv)

    def deliver(i, a):
        s = (z + far(i)) % LINE
        wait_for(ybuf.at[s, a], y_recv.at[s, a])
        zbuf[s, a] = dot(back[s], ybuf[s, a]).astype(BF16)

        @pl.when(i < LINE - 1)
        def _():
            pltpu.make_async_remote_copy(
                src_ref=zbuf.at[s, a], dst_ref=results[a].at[:, lanes(z)],
                send_sem=o_send.at[s], recv_sem=o_recv.at[z],
                device_id={"seq": s * LINE + r}, device_id_type=MESH,
            ).start()

        @pl.when(i == LINE - 1)
        def _():
            pltpu.make_async_copy(
                zbuf.at[z, a], results[a].at[:, lanes(z)], o_recv.at[z]
            ).start()

    def ahead(i, _):
        forward(x, out, top, inv, 2 * i)
        arrive_g(i)
        forward(x, out, top, inv, 2 * i + 1)
        return 0

    lax.fori_loop(0, 4, ahead, 0)

    def between(i, _):
        arrive_g(i + 4)
        spread(i, 0)
        return 0

    lax.fori_loop(0, 4, between, 0)
    regroup(LINE - 1, (3,))

    def behind(i, _):
        @pl.when(i < 4)
        def _():
            spread(i + 4, 0)

        deliver(i, 0)
        backward(x, out, top, inv, dk_acc, dv_acc, i)
        return 0

    lax.fori_loop(0, LINE, behind, 0)

    for i in range(AHEAD):
        for a in range(1, 4):
            spread(i, a)

    def leave(i, _):
        @pl.when(i + AHEAD < LINE)
        def _():
            for a in range(1, 4):
                spread(i + AHEAD, a)

        for a in range(1, 4):
            deliver(i, a)
        return 0

    lax.fori_loop(0, LINE, leave, 0)

    for a in range(4):
        def drain_y(i, _):
            wait_for(xsrc.at[i, a, pl.ds(0, SLOTS - PIECE)], y_send.at[i, a])
            return 0

        lax.fori_loop(0, LINE, drain_y, 0)

    def drain_z(i, _):
        wait_for(zbuf.at[i], o_recv.at[i])

        @pl.when(i != z)
        def _():
            wait_for(zbuf.at[i], o_send.at[i])

        @pl.when(i > 0)
        def _():
            wait_for(zbuf.at[i], z_send.at[i])
            wait_for(zlab.at[i], l_send)

        return 0

    lax.fori_loop(0, LINE, drain_z, 0)


def regroup_order():
    to = np.arange(HALF)
    source = (to % RUN) // MOST * PIECE + to // RUN * MOST + to % MOST
    return (to[None, :] == source[:, None]).astype(np.float32)


def per_device(queries, keys, values, grad_out, cluster):
    dma = pltpu.SemaphoreType.DMA
    labels = cluster.reshape(HEADS, 1, ROWS)
    order = regroup_order()
    return pl.pallas_call(
        kernel,
        out_shape=[jax.ShapeDtypeStruct((ROWS, HEADS * DIM), BF16)] * 4,
        in_specs=[pl.BlockSpec(memory_space=ANY)] * 4 + [pl.BlockSpec(memory_space=VMEM)] * 3,
        out_specs=[pl.BlockSpec(memory_space=ANY)] * 4,
        scratch_shapes=[
            VMEM((LINE, 4, ROWS, DIM), BF16),
            VMEM((LINE, 1, ROWS), jnp.int32),
            VMEM((LINE, SLOTS, ROWS), BF16),
            VMEM((LINE, ROWS, SLOTS), BF16),
            VMEM((LINE, 4, SLOTS, DIM), BF16),
            VMEM((LINE, 4, SLOTS, DIM), BF16),
            VMEM((LINE, 4, SLOTS, DIM), BF16),
            VMEM((OWNED, 4, CAP, DIM), BF16),
            VMEM((OWNED, CAP, DIM), BF16),
            VMEM((OWNED, 1, CAP), F32),
            VMEM((OWNED, 1, CAP), F32),
            VMEM((CAP, DIM), F32),
            VMEM((CAP, DIM), F32),
            dma((LINE,)), dma((LINE, 4)), dma, dma((LINE,)),
            dma((LINE, 4)), dma((LINE, 4)), dma((LINE, 4)), dma((LINE, 4)),
            dma((LINE,)), dma((LINE,)),
        ],
        compiler_params=pltpu.CompilerParams(
            collective_id=0, has_side_effects=True, vmem_limit_bytes=58 * 2**20
        ),
        name="attention",
    )(queries, keys, values, grad_out, labels, jnp.asarray(order, BF16), jnp.asarray(order.T, BF16))


def solution(mesh):
    return jax.shard_map(
        per_device,
        mesh=mesh,
        in_specs=(
            P(("grp", "seq"), None),
            P(("grp", "seq"), None),
            P(("grp", "seq"), None),
            P(("grp", "seq"), None),
            P(None, ("grp", "seq"), None),
        ),
        out_specs=(P(("grp", "seq"), None),) * 4,
        check_vma=False,
    )
```

```python
import jax
import jax.numpy as jnp
import numpy as np
from jax import lax
from jax.experimental import pallas as pl
from jax.experimental.pallas import tpu as pltpu
from jax.sharding import PartitionSpec as P

MESH = pl.DeviceIdType.MESH
HEADS = 8
DIM = 128
ROWS = 384
CLUSTERS = 64
MOST = 12
LINE = 8
OWNED = 8
PIECE = OWNED * MOST
SLOTS = LINE * PIECE
CAP = LINE * LINE * MOST
HALF = SLOTS // 2
RUN = HALF // OWNED
WINDOW = 6
AHEAD = 4
ABSENT = 64.0
NEG = -1e30
SCALE = DIM ** -0.5
LOG2E = 1.4426950408889634
BLOCK_FWD = 384
BLOCK_BWD = 256
F32, BF16 = jnp.float32, jnp.bfloat16
NT = (((1,), (1,)), ((), ()))
VMEM = pltpu.VMEM
ANY = pl.ANY


def inward(n):
    m = n - LINE // 2
    pair, late = m // 6 + 1, (n - 25) // 2 + 1
    dist = jnp.where(
        n < 4, 0,
        jnp.where(
            n < 22, jnp.where(m % 2 == 0, pair, LINE - pair),
            jnp.where(
                (n < 25) | (n == 31), 4, jnp.where(n % 2 == 1, late, LINE - late)
            ),
        ),
    )
    a = jnp.where(n < 4, n, jnp.where(n < 22, m % 6 // 2, jnp.where(n < 25, n - 22, 3)))
    return dist, a


def far(i):
    return jnp.where(i % 2 == 1, 4 - (i + 1) // 2, 4 + i // 2)


def outward(n):
    m = n - 3
    pair = 3 - m // 6
    dist = jnp.where(
        n < 3, 4, jnp.where(n < 21, jnp.where(m % 2 == 0, pair, LINE - pair), 0)
    )
    a = jnp.where(n < 3, n + 1, jnp.where(n < 21, m % 6 // 2 + 1, n - 20))
    return dist, a


def wait_for(ref, sem):
    pltpu.make_async_copy(ref, ref, sem).wait()


def piece(o):
    return pl.ds(pl.multiple_of(o * PIECE, PIECE), PIECE)


def lanes(h):
    return pl.ds(pl.multiple_of(h * DIM, DIM), DIM)


def dot(a, b):
    return jnp.dot(a, b, preferred_element_type=F32)


def dot_nt(a, b):
    return lax.dot_general(a, b, NT, preferred_element_type=F32)


def mask(m):
    return m.astype(F32).astype(BF16)


def scores(k, q, bias, lo, hi):
    t = dot_nt(k[:hi], q) * (SCALE * LOG2E) + bias[:hi]
    late = (
        lax.broadcasted_iota(jnp.int32, (hi - lo, hi - lo), 0)
        > lax.broadcasted_iota(jnp.int32, (hi - lo, hi - lo), 1)
    )
    own = jnp.where(late, NEG, t[lo:hi])
    return jnp.concatenate([t[:lo], own], axis=0) if lo else own


def forward(x, o_ref, top_ref, inv_ref, j):
    k, vt = x[j, 1], x[j, 2].T
    bias = jnp.where(k[:, 0:1].astype(F32) > ABSENT / 2, NEG, 0.0)
    for lo in range(0, CAP, BLOCK_FWD):
        hi = lo + BLOCK_FWD
        t = scores(k, x[j, 0, lo:hi], bias, lo, hi)
        top = jnp.max(t, axis=0, keepdims=True)
        powered = jnp.exp2(t - top)
        inv = 1.0 / jnp.sum(powered, axis=0, keepdims=True)
        top_ref[j, :, lo:hi] = top
        inv_ref[j, :, lo:hi] = inv
        o_ref[j, lo:hi] = dot(vt[:, :hi], (powered * inv).astype(BF16)).T.astype(BF16)


def backward(x, o_ref, top_ref, inv_ref, dk_acc, dv_acc, j):
    k, v = x[j, 1], x[j, 2]
    kt = k.T
    bias = jnp.where(k[:, 0:1].astype(F32) > ABSENT / 2, NEG, 0.0)
    for lo in range(0, CAP, BLOCK_BWD):
        hi = lo + BLOCK_BWD
        q, g = x[j, 0, lo:hi], x[j, 3, lo:hi]
        t = scores(k, q, bias, lo, hi)
        weights = jnp.exp2(t - top_ref[j, :, lo:hi]) * inv_ref[j, :, lo:hi]
        dv = dot(weights.astype(BF16), g)
        row_dot = jnp.sum(
            (g.astype(F32) * o_ref[j, lo:hi].astype(F32)).T, axis=0, keepdims=True
        )
        ds = (weights * (dot_nt(v[:hi], g) - row_dot)).astype(BF16)
        dk = dot(ds, q)
        x[j, 0, lo:hi] = (dot(kt[:, :hi], ds) * SCALE).T.astype(BF16)
        if lo:
            dk_acc[:lo] += dk[:lo]
            dv_acc[:lo] += dv[:lo]
        dk_acc[lo:hi] = dk[lo:]
        dv_acc[lo:hi] = dv[lo:]
    x[j, 1] = (dk_acc[...] * SCALE).astype(BF16)
    x[j, 2] = dv_acc[...].astype(BF16)


def kernel(
    q_ref, k_ref, v_ref, g_ref, label_ref, order_ref, undo_ref,
    o_ref, dq_ref, dk_ref, dv_ref,
    zbuf, zlab, pick, back, xsrc, xbuf, ybuf, x, out, top, inv, dk_acc, dv_acc,
    z_send, z_recv, l_send, l_recv, x_send, x_recv, y_send, y_recv, o_send, o_recv,
):
    me = lax.axis_index("seq")
    z, r = me // LINE, me % LINE
    sources = (q_ref, k_ref, v_ref, g_ref)
    results = (o_ref, dq_ref, dk_ref, dv_ref)

    barrier = pltpu.get_barrier_semaphore()
    for i in range(1, LINE):
        pl.semaphore_signal(
            barrier, inc=1, device_id={"seq": lax.rem(z + i, LINE) * LINE + r}, device_id_type=MESH
        )
        pl.semaphore_signal(
            barrier, inc=1, device_id={"seq": z * LINE + lax.rem(r + i, LINE)}, device_id_type=MESH
        )

    pltpu.make_async_copy(label_ref.at[z], zlab.at[z], l_recv.at[z]).start()
    for a in range(4):
        pltpu.make_async_copy(
            sources[a].at[:, lanes(z)], zbuf.at[z, a], z_recv.at[z, a]
        ).start()

    before = mask(
        lax.broadcasted_iota(jnp.int32, (ROWS, ROWS), 0)
        < lax.broadcasted_iota(jnp.int32, (ROWS, ROWS), 1)
    )

    def prepare(s):
        wait_for(zlab.at[s], l_recv.at[s])
        label = zlab[s]
        named = (
            lax.broadcasted_iota(jnp.int32, (CLUSTERS, ROWS), 0) == label
        ).astype(F32)
        rank = jnp.sum(named * dot(named.astype(BF16), before), axis=0, keepdims=True)
        slot = label * MOST + rank.astype(jnp.int32)
        pick[s] = mask(lax.broadcasted_iota(jnp.int32, (SLOTS, ROWS), 0) == slot)
        column = jnp.broadcast_to(slot.astype(F32), (DIM, ROWS)).T[:, 0:1].astype(jnp.int32)
        back[s] = mask(lax.broadcasted_iota(jnp.int32, (ROWS, SLOTS), 1) == column)

    prepare(z)
    pl.semaphore_wait(barrier, 2 * (LINE - 1))

    def send_z(n, _):
        dist, at = inward(n)
        to = (z + dist) % LINE
        for a in range(4):
            @pl.when(at == a)
            def _():
                pltpu.make_async_remote_copy(
                    src_ref=sources[a].at[:, lanes(to)], dst_ref=zbuf.at[z, a],
                    send_sem=z_send.at[dist], recv_sem=z_recv.at[z, a],
                    device_id={"seq": to * LINE + r}, device_id_type=MESH,
                ).start()
        return 0

    def send_label(i, _):
        to = (z + i) % LINE
        pltpu.make_async_remote_copy(
            src_ref=label_ref.at[to], dst_ref=zlab.at[z], send_sem=l_send, recv_sem=l_recv.at[z],
            device_id={"seq": to * LINE + r}, device_id_type=MESH,
        ).start()
        return 0

    lax.fori_loop(1, LINE, send_label, 0)
    lax.fori_loop(4, 4 + WINDOW, send_z, 0)

    def to_owners(s, a, buf, send_sem, recv_sem):
        pltpu.make_async_copy(
            xsrc.at[s, a, piece(r)], buf.at[s, a, piece(r)], recv_sem.at[s, a]
        ).start()

        def send(n, _):
            o = (r + n) % LINE
            pltpu.make_async_remote_copy(
                src_ref=xsrc.at[s, a, piece(o)], dst_ref=buf.at[s, a, piece(r)],
                send_sem=send_sem.at[s, a], recv_sem=recv_sem.at[s, a],
                device_id={"seq": z * LINE + o}, device_id_type=MESH,
            ).start()
            return 0

        lax.fori_loop(1, LINE, send, 0)

    def pack(n, _):
        dist, a = inward(n)
        s = (z - dist + LINE) % LINE

        @pl.when((a == 0) & (n > 0))
        def _():
            prepare(s)

        wait_for(zbuf.at[s, a], z_recv.at[s, a])
        xsrc[s, a] = dot(pick[s], zbuf[s, a]).astype(BF16)

        @pl.when(a == 1)
        def _():
            used = jnp.sum(pick[s].astype(F32), axis=1, keepdims=True)
            first = lax.broadcasted_iota(jnp.int32, (SLOTS, DIM), 1) == 0
            mark = jnp.where(first, (1.0 - used) * ABSENT, 0.0)
            xsrc[s, 1] = (xsrc[s, 1].astype(F32) + mark).astype(BF16)

        to_owners(s, a, xbuf, x_send, x_recv)

        @pl.when((n + WINDOW >= 4 + WINDOW) & (n + WINDOW < 32))
        def _():
            send_z(n + WINDOW, 0)

        return 0

    def regroup(n, _):
        dist, a = inward(n)
        s = (z - dist + LINE) % LINE
        wait_for(xbuf.at[s, a], x_recv.at[s, a])
        for half in range(2):
            moved = dot(
                order_ref[...], xbuf[s, a, half * HALF:(half + 1) * HALF]
            ).astype(BF16)
            for j in range(OWNED):
                at = pl.multiple_of(s * PIECE + half * RUN, 16)
                x[j, a, pl.ds(at, RUN), :] = moved[j * RUN:(j + 1) * RUN]
        return 0

    def arrive(n, _):
        pack(n, 0)
        lo = jnp.where(n < 16, jnp.maximum(n - 7, 0), 9 + (3 * (n - 16) + 1) // 2)
        hi = jnp.where(n < 16, jnp.maximum(n - 6, 0), lo + 2 - n % 2)
        lax.fori_loop(lo, hi, regroup, 0)
        return 0

    def spread(s, a, taken):
        wait_for(xsrc.at[s, a, pl.ds(0, SLOTS - PIECE)], x_send.at[s, a])
        for half in range(2):
            at = pl.multiple_of(s * PIECE + half * RUN, 16)
            rows = jnp.concatenate([taken(j, pl.ds(at, RUN)) for j in range(OWNED)], axis=0)
            xsrc[s, a, half * HALF:(half + 1) * HALF] = dot(undo_ref[...], rows).astype(BF16)
        to_owners(s, a, ybuf, y_send, y_recv)

    def spread_out(i, _):
        spread((z + far(i)) % LINE, 0, lambda j, rows: out[j, rows, :])
        return 0

    def spread_grad(n, _):
        dist, a = outward(n)
        spread((z + dist) % LINE, a, lambda j, rows: x[j, a - 1, rows, :])
        return 0

    def deliver(s, at, arrays):
        wait_for(ybuf.at[s, at], y_recv.at[s, at])
        zbuf[s, at] = dot(back[s], ybuf[s, at]).astype(BF16)
        for a in arrays:
            @pl.when((at == a) & (s != z))
            def _():
                pltpu.make_async_remote_copy(
                    src_ref=zbuf.at[s, a], dst_ref=results[a].at[:, lanes(z)],
                    send_sem=o_send.at[s], recv_sem=o_recv.at[z],
                    device_id={"seq": s * LINE + r}, device_id_type=MESH,
                ).start()

            @pl.when((at == a) & (s == z))
            def _():
                pltpu.make_async_copy(
                    zbuf.at[z, a], results[a].at[:, lanes(z)], o_recv.at[z]
                ).start()

    lax.fori_loop(0, 25, arrive, 0)
    lax.fori_loop(25, 27, pack, 0)
    lax.fori_loop(23, 25, regroup, 0)

    def ahead(i, _):
        forward(x, out, top, inv, 2 * i)
        forward(x, out, top, inv, 2 * i + 1)
        lo = jnp.where(i == 0, 27, jnp.where(i < 3, 29, 31))
        hi = jnp.where(i < 2, 29, jnp.where(i == 2, 31, 32))
        lax.fori_loop(lo, hi, pack, 0)
        lo = jnp.where(i < 2, 25, 27)
        hi = jnp.where(i == 0, 25, jnp.where(i < 3, 27, 29))
        lax.fori_loop(lo, hi, regroup, 0)
        return 0

    lax.fori_loop(0, 4, ahead, 0)
    lax.fori_loop(0, 3, spread_out, 0)
    lax.fori_loop(29, 32, regroup, 0)

    def behind(i, _):
        backward(x, out, top, inv, dk_acc, dv_acc, i)
        deliver((z + far(i)) % LINE, 0, (0,))

        @pl.when(i + 3 < LINE)
        def _():
            spread_out(i + 3, 0)

        return 0

    lax.fori_loop(0, LINE, behind, 0)
    lax.fori_loop(0, AHEAD, spread_grad, 0)

    def leave(n, _):
        @pl.when(n + AHEAD < 24)
        def _():
            spread_grad(n + AHEAD, 0)

        dist, a = outward(n)
        deliver((z + dist) % LINE, a, (1, 2, 3))
        return 0

    lax.fori_loop(0, 24, leave, 0)

    def drain(i, _):
        wait_for(zbuf.at[i], o_recv.at[i])
        for a in range(4):
            wait_for(xsrc.at[i, a, pl.ds(0, SLOTS - PIECE)], y_send.at[i, a])

        @pl.when(i != z)
        def _():
            wait_for(zbuf.at[i], o_send.at[i])

        @pl.when(i > 0)
        def _():
            wait_for(zbuf.at[i], z_send.at[i])
            wait_for(zlab.at[i], l_send)

        return 0

    lax.fori_loop(0, LINE, drain, 0)


def regroup_order():
    to = np.arange(HALF)
    source = (to % RUN) // MOST * PIECE + to // RUN * MOST + to % MOST
    return (to[None, :] == source[:, None]).astype(np.float32)


def per_device(queries, keys, values, grad_out, cluster):
    dma = pltpu.SemaphoreType.DMA
    labels = cluster.reshape(HEADS, 1, ROWS)
    order = regroup_order()
    return pl.pallas_call(
        kernel,
        out_shape=[jax.ShapeDtypeStruct((ROWS, HEADS * DIM), BF16)] * 4,
        in_specs=[pl.BlockSpec(memory_space=ANY)] * 4 + [pl.BlockSpec(memory_space=VMEM)] * 3,
        out_specs=[pl.BlockSpec(memory_space=ANY)] * 4,
        scratch_shapes=[
            VMEM((LINE, 4, ROWS, DIM), BF16),
            VMEM((LINE, 1, ROWS), jnp.int32),
            VMEM((LINE, SLOTS, ROWS), BF16),
            VMEM((LINE, ROWS, SLOTS), BF16),
            VMEM((LINE, 4, SLOTS, DIM), BF16),
            VMEM((LINE, 4, SLOTS, DIM), BF16),
            VMEM((LINE, 4, SLOTS, DIM), BF16),
            VMEM((OWNED, 4, CAP, DIM), BF16),
            VMEM((OWNED, CAP, DIM), BF16),
            VMEM((OWNED, 1, CAP), F32),
            VMEM((OWNED, 1, CAP), F32),
            VMEM((CAP, DIM), F32),
            VMEM((CAP, DIM), F32),
            dma((LINE,)), dma((LINE, 4)), dma, dma((LINE,)),
            dma((LINE, 4)), dma((LINE, 4)), dma((LINE, 4)), dma((LINE, 4)),
            dma((LINE,)), dma((LINE,)),
        ],
        compiler_params=pltpu.CompilerParams(
            collective_id=0, has_side_effects=True, vmem_limit_bytes=58 * 2**20
        ),
        name="attention",
    )(queries, keys, values, grad_out, labels, jnp.asarray(order, BF16), jnp.asarray(order.T, BF16))


def solution(mesh):
    return jax.shard_map(
        per_device,
        mesh=mesh,
        in_specs=(
            P(("grp", "seq"), None),
            P(("grp", "seq"), None),
            P(("grp", "seq"), None),
            P(("grp", "seq"), None),
            P(None, ("grp", "seq"), None),
        ),
        out_specs=(P(("grp", "seq"), None),) * 4,
        check_vma=False,
    )
```

```python
import jax
import jax.numpy as jnp
import numpy as np
from jax import lax
from jax.experimental import pallas as pl
from jax.experimental.pallas import tpu as pltpu
from jax.sharding import PartitionSpec as P

MESH = pl.DeviceIdType.MESH
HEADS = 8
DIM = 128
ROWS = 384
CLUSTERS = 64
MOST = 12
LINE = 8
OWNED = 8
PIECE = OWNED * MOST
SLOTS = LINE * PIECE
CAP = LINE * LINE * MOST
HALF = SLOTS // 2
RUN = HALF // OWNED
WINDOW = 6
AHEAD = 6
PARTS = 3
ABSENT = 64.0
NEG = -1e30
SCALE = DIM ** -0.5
LOG2E = 1.4426950408889634
BLOCK_FWD = 384
BLOCK_BWD = 256
F32, BF16 = jnp.float32, jnp.bfloat16
NT = (((1,), (1,)), ((), ()))
VMEM = pltpu.VMEM
ANY = pl.ANY


def inward(n):
    m = n - 4
    pair, late = m // 4 + 1, (n - 18) % 7
    signed = jnp.where(m % 2 == 0, pair, LINE - pair)
    alone = jnp.where(
        late == 6, 4, jnp.where(late % 2 == 0, late // 2 + 1, LINE - 1 - late // 2)
    )
    dist = jnp.where(
        n < 4, 0, jnp.where(n < 16, signed, jnp.where(n < 18, 4, alone))
    )
    a = jnp.where(
        n < 4, n, jnp.where(n < 16, m % 4 // 2, jnp.where(n < 18, n - 16, jnp.where(n < 25, 2, 3)))
    )
    return dist, a


def outward(n):
    i, m = n % LINE, n - 18
    pair = 3 - m // 4
    alone = jnp.where(i % 2 == 1, 4 - (i + 1) // 2, 4 + i // 2)
    signed = jnp.where(m % 2 == 0, pair, LINE - pair)
    dist = jnp.where(
        n < 16, alone, jnp.where(n < 18, 4, jnp.where(n < 30, signed, 0))
    )
    a = jnp.where(
        n < 8, 0,
        jnp.where(n < 16, 3, jnp.where(n < 18, n - 15, jnp.where(n < 30, m % 4 // 2 + 1, n - 29))),
    )
    return dist, a


def wait_for(ref, sem):
    pltpu.make_async_copy(ref, ref, sem).wait()


def piece(o):
    return pl.ds(pl.multiple_of(o * PIECE, PIECE), PIECE)


def lanes(h):
    return pl.ds(pl.multiple_of(h * DIM, DIM), DIM)


def dot(a, b):
    return jnp.dot(a, b, preferred_element_type=F32)


def dot_nt(a, b):
    return lax.dot_general(a, b, NT, preferred_element_type=F32)


def mask(m):
    return m.astype(F32).astype(BF16)


def scores(k, q, bias, lo, hi):
    t = dot_nt(k[:hi], q) * (SCALE * LOG2E) + bias[:hi]
    late = (
        lax.broadcasted_iota(jnp.int32, (hi - lo, hi - lo), 0)
        > lax.broadcasted_iota(jnp.int32, (hi - lo, hi - lo), 1)
    )
    own = jnp.where(late, NEG, t[lo:hi])
    return jnp.concatenate([t[:lo], own], axis=0) if lo else own


def softmax(x, weights, top_ref, inv_ref, j):
    k = x[j, 1]
    bias = jnp.where(k[:, 0:1].astype(F32) > ABSENT / 2, NEG, 0.0)
    at = 0
    for lo in range(0, CAP, BLOCK_FWD):
        hi = lo + BLOCK_FWD
        t = scores(k, x[j, 0, lo:hi], bias, lo, hi)
        top = jnp.max(t, axis=0, keepdims=True)
        powered = jnp.exp2(t - top)
        inv = 1.0 / jnp.sum(powered, axis=0, keepdims=True)
        top_ref[j, :, lo:hi] = top
        inv_ref[j, :, lo:hi] = inv
        weights[j, at:at + hi] = (powered * inv).astype(BF16)
        at += hi


def attend(x, y, weights, j):
    vt = x[j, 2].T
    at = 0
    for hi in range(BLOCK_FWD, CAP + 1, BLOCK_FWD):
        y[j, 0, hi - BLOCK_FWD:hi] = dot(vt[:, :hi], weights[j, at:at + hi]).T.astype(BF16)
        at += hi


def value_gradient(x, y, weights, j):
    g = x[j, 3]
    half = BLOCK_FWD
    y[j, 3, :half] = (
        dot(weights[j, :half], g[:half]) + dot(weights[j, half:2 * half], g[half:])
    ).astype(BF16)
    y[j, 3, half:] = dot(weights[j, 2 * half:], g[half:]).astype(BF16)


def backward(x, y, top_ref, inv_ref, dk_acc, j):
    k, v = x[j, 1], x[j, 2]
    kt = k.T
    bias = jnp.where(k[:, 0:1].astype(F32) > ABSENT / 2, NEG, 0.0)
    for lo in range(0, CAP, BLOCK_BWD):
        hi = lo + BLOCK_BWD
        q, g = x[j, 0, lo:hi], x[j, 3, lo:hi]
        t = scores(k, q, bias, lo, hi)
        weights = jnp.exp2(t - top_ref[j, :, lo:hi]) * inv_ref[j, :, lo:hi]
        row_dot = jnp.sum(
            (g.astype(F32) * y[j, 0, lo:hi].astype(F32)).T, axis=0, keepdims=True
        )
        ds = (weights * (dot_nt(v[:hi], g) - row_dot)).astype(BF16)
        dk = dot(ds, q)
        y[j, 1, lo:hi] = (dot(kt[:, :hi], ds) * SCALE).T.astype(BF16)
        if lo:
            dk_acc[:lo] += dk[:lo]
        dk_acc[lo:hi] = dk[lo:]
    y[j, 2] = (dk_acc[...] * SCALE).astype(BF16)


def kernel(
    q_ref, k_ref, v_ref, g_ref, label_ref, order_ref, undo_ref,
    o_ref, dq_ref, dk_ref, dv_ref,
    zbuf, zlab, pick, back, xsrc, xbuf, ybuf, x, y, weights, top, inv, dk_acc,
    z_send, z_recv, l_send, l_recv, x_send, x_recv, y_send, y_recv, o_send, o_recv,
):
    me = lax.axis_index("seq")
    z, r = me // LINE, me % LINE
    sources = (q_ref, k_ref, v_ref, g_ref)
    results = (o_ref, dq_ref, dk_ref, dv_ref)

    barrier = pltpu.get_barrier_semaphore()
    for i in range(1, LINE):
        pl.semaphore_signal(
            barrier, inc=1, device_id={"seq": lax.rem(z + i, LINE) * LINE + r}, device_id_type=MESH
        )
        pl.semaphore_signal(
            barrier, inc=1, device_id={"seq": z * LINE + lax.rem(r + i, LINE)}, device_id_type=MESH
        )

    pltpu.make_async_copy(label_ref.at[z], zlab.at[z], l_recv.at[z]).start()
    for a in range(4):
        pltpu.make_async_copy(
            sources[a].at[:, lanes(z)], zbuf.at[z, a], z_recv.at[z, a]
        ).start()

    before = mask(
        lax.broadcasted_iota(jnp.int32, (ROWS, ROWS), 0)
        < lax.broadcasted_iota(jnp.int32, (ROWS, ROWS), 1)
    )

    def prepare(s):
        wait_for(zlab.at[s], l_recv.at[s])
        label = zlab[s]
        named = (
            lax.broadcasted_iota(jnp.int32, (CLUSTERS, ROWS), 0) == label
        ).astype(F32)
        rank = jnp.sum(named * dot(named.astype(BF16), before), axis=0, keepdims=True)
        slot = label * MOST + rank.astype(jnp.int32)
        pick[s] = mask(lax.broadcasted_iota(jnp.int32, (SLOTS, ROWS), 0) == slot)
        column = jnp.broadcast_to(slot.astype(F32), (DIM, ROWS)).T[:, 0:1].astype(jnp.int32)
        back[s] = mask(lax.broadcasted_iota(jnp.int32, (ROWS, SLOTS), 1) == column)

    prepare(z)
    pl.semaphore_wait(barrier, 2 * (LINE - 1))

    def send_z(n, _):
        dist, at = inward(n)
        to = (z + dist) % LINE
        for a in range(4):
            @pl.when(at == a)
            def _():
                pltpu.make_async_remote_copy(
                    src_ref=sources[a].at[:, lanes(to)], dst_ref=zbuf.at[z, a],
                    send_sem=z_send.at[dist], recv_sem=z_recv.at[z, a],
                    device_id={"seq": to * LINE + r}, device_id_type=MESH,
                ).start()
        return 0

    def send_label(i, _):
        to = (z + i) % LINE
        pltpu.make_async_remote_copy(
            src_ref=label_ref.at[to], dst_ref=zlab.at[z], send_sem=l_send, recv_sem=l_recv.at[z],
            device_id={"seq": to * LINE + r}, device_id_type=MESH,
        ).start()
        return 0

    lax.fori_loop(1, LINE, send_label, 0)
    lax.fori_loop(4, 4 + WINDOW, send_z, 0)

    def to_owners(s, a, buf, send_sem, recv_sem):
        pltpu.make_async_copy(
            xsrc.at[s, a, piece(r)], buf.at[s, a, piece(r)], recv_sem.at[s, a]
        ).start()

        def send(n, _):
            o = (r + n) % LINE
            pltpu.make_async_remote_copy(
                src_ref=xsrc.at[s, a, piece(o)], dst_ref=buf.at[s, a, piece(r)],
                send_sem=send_sem.at[s, a], recv_sem=recv_sem.at[s, a],
                device_id={"seq": z * LINE + o}, device_id_type=MESH,
            ).start()
            return 0

        lax.fori_loop(1, LINE, send, 0)

    def pack(n, _):
        dist, a = inward(n)
        s = (z - dist + LINE) % LINE

        @pl.when((a == 0) & (n > 0))
        def _():
            prepare(s)

        wait_for(zbuf.at[s, a], z_recv.at[s, a])
        xsrc[s, a] = dot(pick[s], zbuf[s, a]).astype(BF16)

        @pl.when(a == 1)
        def _():
            used = jnp.sum(pick[s].astype(F32), axis=1, keepdims=True)
            first = lax.broadcasted_iota(jnp.int32, (SLOTS, DIM), 1) == 0
            mark = jnp.where(first, (1.0 - used) * ABSENT, 0.0)
            xsrc[s, 1] = (xsrc[s, 1].astype(F32) + mark).astype(BF16)

        to_owners(s, a, xbuf, x_send, x_recv)

        @pl.when((n + WINDOW >= 4 + WINDOW) & (n + WINDOW < 32))
        def _():
            send_z(n + WINDOW, 0)

        return 0

    def regroup(n, _):
        dist, a = inward(n)
        s = (z - dist + LINE) % LINE
        wait_for(xbuf.at[s, a], x_recv.at[s, a])
        for half in range(2):
            moved = dot(
                order_ref[...], xbuf[s, a, half * HALF:(half + 1) * HALF]
            ).astype(BF16)
            for j in range(OWNED):
                at = pl.multiple_of(s * PIECE + half * RUN, 16)
                x[j, a, pl.ds(at, RUN), :] = moved[j * RUN:(j + 1) * RUN]
        return 0

    def arrive(n, _):
        pack(n, 0)
        lo = jnp.where(n < 14, jnp.maximum(n - 7, 0), 7 + (3 * (n - 14) + 1) // 2)
        hi = jnp.where(n < 14, jnp.maximum(n - 6, 0), lo + 2 - n % 2)
        lax.fori_loop(lo, hi, regroup, 0)
        return 0

    def spread(n, _):
        dist, a = outward(n)
        s = (z + dist) % LINE
        wait_for(xsrc.at[s, a, pl.ds(0, SLOTS - PIECE)], x_send.at[s, a])
        for half in range(2):
            at = pl.multiple_of(s * PIECE + half * RUN, 16)
            rows = jnp.concatenate([y[j, a, pl.ds(at, RUN), :] for j in range(OWNED)], axis=0)
            xsrc[s, a, half * HALF:(half + 1) * HALF] = dot(undo_ref[...], rows).astype(BF16)
        to_owners(s, a, ybuf, y_send, y_recv)
        return 0

    def deliver(n, _):
        dist, at = outward(n)
        s = (z + dist) % LINE
        wait_for(ybuf.at[s, at], y_recv.at[s, at])
        zbuf[s, at] = dot(back[s], ybuf[s, at]).astype(BF16)
        for a in range(4):
            @pl.when((at == a) & (s != z))
            def _():
                pltpu.make_async_remote_copy(
                    src_ref=zbuf.at[s, a], dst_ref=results[a].at[:, lanes(z)],
                    send_sem=o_send.at[s], recv_sem=o_recv.at[z],
                    device_id={"seq": s * LINE + r}, device_id_type=MESH,
                ).start()

            @pl.when((at == a) & (s == z))
            def _():
                pltpu.make_async_copy(
                    zbuf.at[z, a], results[a].at[:, lanes(z)], o_recv.at[z]
                ).start()
        return 0

    lax.fori_loop(0, 18, arrive, 0)
    lax.fori_loop(18, 20, pack, 0)
    lax.fori_loop(13, 18, regroup, 0)
    lax.fori_loop(20, 22, pack, 0)

    def score(i, _):
        softmax(x, weights, top, inv, 2 * i)
        softmax(x, weights, top, inv, 2 * i + 1)
        lo = jnp.where(i < 3, 22, 24)
        hi = jnp.where(i < 2, 22, jnp.where(i < 3, 24, 25))
        lax.fori_loop(lo, hi, pack, 0)
        regroup(18 + i, 0)
        return 0

    lax.fori_loop(0, 4, score, 0)
    lax.fori_loop(25, 27, pack, 0)
    lax.fori_loop(22, 25, regroup, 0)

    def attend_one(j, _):
        attend(x, y, weights, j)
        return 0

    lax.fori_loop(0, OWNED, attend_one, 0)
    lax.fori_loop(0, 3, spread, 0)
    lax.fori_loop(27, 29, pack, 0)
    deliver(0, 0)
    lax.fori_loop(25, 27, regroup, 0)
    deliver(1, 0)
    lax.fori_loop(29, 31, pack, 0)
    deliver(2, 0)
    pack(31, 0)
    lax.fori_loop(3, 5, spread, 0)
    lax.fori_loop(27, 32, regroup, 0)

    def value_one(j, _):
        value_gradient(x, y, weights, j)

        @pl.when(j < 3)
        def _():
            spread(j + 5, 0)

        @pl.when(j % 4 == 3)
        def _():
            deliver(3 + j // 4, 0)

        return 0

    lax.fori_loop(0, OWNED, value_one, 0)
    lax.fori_loop(8, 10, spread, 0)

    def behind(i, _):
        backward(x, y, top, inv, dk_acc, i)
        deliver(i + 5, 0)

        @pl.when(i < 6)
        def _():
            spread(i + 10, 0)

        return 0

    lax.fori_loop(0, OWNED, behind, 0)
    lax.fori_loop(16, 13 + AHEAD, spread, 0)

    def leave(n, _):
        @pl.when(n + AHEAD < 32)
        def _():
            spread(n + AHEAD, 0)

        deliver(n, 0)
        return 0

    lax.fori_loop(13, 32, leave, 0)

    def drain(i, _):
        wait_for(zbuf.at[i], o_recv.at[i])
        for a in range(4):
            wait_for(xsrc.at[i, a, pl.ds(0, SLOTS - PIECE)], y_send.at[i, a])

        @pl.when(i != z)
        def _():
            wait_for(zbuf.at[i], o_send.at[i])

        @pl.when(i > 0)
        def _():
            wait_for(zbuf.at[i], z_send.at[i])
            wait_for(zlab.at[i], l_send)

        return 0

    lax.fori_loop(0, LINE, drain, 0)


def regroup_order():
    to = np.arange(HALF)
    source = (to % RUN) // MOST * PIECE + to // RUN * MOST + to % MOST
    return (to[None, :] == source[:, None]).astype(np.float32)


def finish_kernel(*refs):
    for a in range(4):
        refs[4 + a][...] = refs[a][...]


def per_device(queries, keys, values, grad_out, cluster):
    dma = pltpu.SemaphoreType.DMA
    labels = cluster.reshape(HEADS, 1, ROWS)
    order = regroup_order()
    outs = pl.pallas_call(
        kernel,
        out_shape=[jax.ShapeDtypeStruct((ROWS, HEADS * DIM), BF16)] * 4,
        in_specs=[pl.BlockSpec(memory_space=ANY)] * 4 + [pl.BlockSpec(memory_space=VMEM)] * 3,
        out_specs=[pl.BlockSpec(memory_space=ANY)] * 4,
        scratch_shapes=[
            VMEM((LINE, 4, ROWS, DIM), BF16),
            VMEM((LINE, 1, ROWS), jnp.int32),
            VMEM((LINE, SLOTS, ROWS), BF16),
            VMEM((LINE, ROWS, SLOTS), BF16),
            VMEM((LINE, 4, SLOTS, DIM), BF16),
            VMEM((LINE, 4, SLOTS, DIM), BF16),
            VMEM((LINE, 4, SLOTS, DIM), BF16),
            VMEM((OWNED, 4, CAP, DIM), BF16),
            VMEM((OWNED, 4, CAP, DIM), BF16),
            VMEM((OWNED, 3 * BLOCK_FWD, BLOCK_FWD), BF16),
            VMEM((OWNED, 1, CAP), F32),
            VMEM((OWNED, 1, CAP), F32),
            VMEM((CAP, DIM), F32),
            dma((LINE,)), dma((LINE, 4)), dma, dma((LINE,)),
            dma((LINE, 4)), dma((LINE, 4)), dma((LINE, 4)), dma((LINE, 4)),
            dma((LINE,)), dma((LINE,)),
        ],
        compiler_params=pltpu.CompilerParams(
            collective_id=0, has_side_effects=True, vmem_limit_bytes=60 * 2**20
        ),
        name="attention",
    )(queries, keys, values, grad_out, labels, jnp.asarray(order, BF16), jnp.asarray(order.T, BF16))
    spec = pl.BlockSpec((ROWS // PARTS, HEADS * DIM), lambda i: (i, 0))
    return pl.pallas_call(
        finish_kernel,
        grid=(PARTS,),
        out_shape=[jax.ShapeDtypeStruct((ROWS, HEADS * DIM), BF16)] * 4,
        in_specs=[spec] * 4,
        out_specs=[spec] * 4,
        name="finish",
    )(*outs)


def solution(mesh):
    return jax.shard_map(
        per_device,
        mesh=mesh,
        in_specs=(
            P(("grp", "seq"), None),
            P(("grp", "seq"), None),
            P(("grp", "seq"), None),
            P(("grp", "seq"), None),
            P(None, ("grp", "seq"), None),
        ),
        out_specs=(P(("grp", "seq"), None),) * 4,
        check_vma=False,
    )
```

```python
import jax
import jax.numpy as jnp
import numpy as np
from jax import lax
from jax.experimental import pallas as pl
from jax.experimental.pallas import tpu as pltpu
from jax.sharding import PartitionSpec as P

MESH = pl.DeviceIdType.MESH
HEADS = 8
DIM = 128
ROWS = 384
CLUSTERS = 64
MOST = 12
LINE = 8
OWNED = 8
PIECE = OWNED * MOST
SLOTS = LINE * PIECE
CAP = LINE * LINE * MOST
HALF = SLOTS // 2
RUN = HALF // OWNED
WINDOW = 6
AHEAD = 6
ABSENT = 64.0
NEG = -1e30
SCALE = DIM ** -0.5
LOG2E = 1.4426950408889634
BLOCK_FWD = 384
BLOCK_BWD = 256
F32, BF16 = jnp.float32, jnp.bfloat16
NT = (((1,), (1,)), ((), ()))
VMEM = pltpu.VMEM
ANY = pl.ANY


def inward(n):
    m = n - 4
    pair, late = m // 4 + 1, (n - 18) % 7
    signed = jnp.where(m % 2 == 0, pair, LINE - pair)
    alone = jnp.where(
        late == 6, 4, jnp.where(late % 2 == 0, late // 2 + 1, LINE - 1 - late // 2)
    )
    dist = jnp.where(
        n < 4, 0, jnp.where(n < 16, signed, jnp.where(n < 18, 4, alone))
    )
    a = jnp.where(
        n < 4, n, jnp.where(n < 16, m % 4 // 2, jnp.where(n < 18, n - 16, jnp.where(n < 25, 2, 3)))
    )
    return dist, a


def outward(n):
    i, m = n % LINE, n - 18
    pair = 3 - m // 4
    alone = jnp.where(i % 2 == 1, 4 - (i + 1) // 2, 4 + i // 2)
    signed = jnp.where(m % 2 == 0, pair, LINE - pair)
    dist = jnp.where(
        n < 16, alone, jnp.where(n < 18, 4, jnp.where(n < 30, signed, 0))
    )
    a = jnp.where(
        n < 8, 0,
        jnp.where(n < 16, 3, jnp.where(n < 18, n - 15, jnp.where(n < 30, m % 4 // 2 + 1, n - 29))),
    )
    return dist, a


def wait_for(ref, sem):
    pltpu.make_async_copy(ref, ref, sem).wait()


def piece(o):
    return pl.ds(pl.multiple_of(o * PIECE, PIECE), PIECE)


def lanes(h):
    return pl.ds(pl.multiple_of(h * DIM, DIM), DIM)


def dot(a, b):
    return jnp.dot(a, b, preferred_element_type=F32)


def dot_nt(a, b):
    return lax.dot_general(a, b, NT, preferred_element_type=F32)


def mask(m):
    return m.astype(F32).astype(BF16)


def scores(k, q, bias, lo, hi):
    t = dot_nt(k[:hi], q) * (SCALE * LOG2E) + bias[:hi]
    late = (
        lax.broadcasted_iota(jnp.int32, (hi - lo, hi - lo), 0)
        > lax.broadcasted_iota(jnp.int32, (hi - lo, hi - lo), 1)
    )
    own = jnp.where(late, NEG, t[lo:hi])
    return jnp.concatenate([t[:lo], own], axis=0) if lo else own


def softmax(x, weights, top_ref, inv_ref, j):
    k = x[j, 1]
    bias = jnp.where(k[:, 0:1].astype(F32) > ABSENT / 2, NEG, 0.0)
    at = 0
    for lo in range(0, CAP, BLOCK_FWD):
        hi = lo + BLOCK_FWD
        t = scores(k, x[j, 0, lo:hi], bias, lo, hi)
        top = jnp.max(t, axis=0, keepdims=True)
        powered = jnp.exp2(t - top)
        inv = 1.0 / jnp.sum(powered, axis=0, keepdims=True)
        top_ref[j, :, lo:hi] = top
        inv_ref[j, :, lo:hi] = inv
        weights[j, at:at + hi] = (powered * inv).astype(BF16)
        at += hi


def attend(x, y, weights, j):
    vt = x[j, 2].T
    at = 0
    for hi in range(BLOCK_FWD, CAP + 1, BLOCK_FWD):
        y[j, 0, hi - BLOCK_FWD:hi] = dot(vt[:, :hi], weights[j, at:at + hi]).T.astype(BF16)
        at += hi


def value_gradient(x, y, weights, j):
    g = x[j, 3]
    half = BLOCK_FWD
    y[j, 3, :half] = (
        dot(weights[j, :half], g[:half]) + dot(weights[j, half:2 * half], g[half:])
    ).astype(BF16)
    y[j, 3, half:] = dot(weights[j, 2 * half:], g[half:]).astype(BF16)


def backward(x, y, top_ref, inv_ref, dk_acc, j):
    k, v = x[j, 1], x[j, 2]
    kt = k.T
    bias = jnp.where(k[:, 0:1].astype(F32) > ABSENT / 2, NEG, 0.0)
    for lo in range(0, CAP, BLOCK_BWD):
        hi = lo + BLOCK_BWD
        q, g = x[j, 0, lo:hi], x[j, 3, lo:hi]
        t = scores(k, q, bias, lo, hi)
        weights = jnp.exp2(t - top_ref[j, :, lo:hi]) * inv_ref[j, :, lo:hi]
        row_dot = jnp.sum(
            (g.astype(F32) * y[j, 0, lo:hi].astype(F32)).T, axis=0, keepdims=True
        )
        ds = (weights * (dot_nt(v[:hi], g) - row_dot)).astype(BF16)
        dk = dot(ds, q)
        y[j, 1, lo:hi] = (dot(kt[:, :hi], ds) * SCALE).T.astype(BF16)
        if lo:
            dk_acc[:lo] += dk[:lo]
        dk_acc[lo:hi] = dk[lo:]
    y[j, 2] = (dk_acc[...] * SCALE).astype(BF16)


def kernel(
    q_ref, k_ref, v_ref, g_ref, label_ref, order_ref, undo_ref,
    o_ref, dq_ref, dk_ref, dv_ref,
    zbuf, zlab, pick, back, xsrc, xbuf, ybuf, x, y, weights, top, inv, dk_acc,
    z_send, z_recv, l_send, l_recv, x_send, x_recv, y_send, y_recv, o_send, o_recv,
):
    me = lax.axis_index("seq")
    z, r = me // LINE, me % LINE
    sources = (q_ref, k_ref, v_ref, g_ref)
    results = (o_ref, dq_ref, dk_ref, dv_ref)

    barrier = pltpu.get_barrier_semaphore()
    for i in range(1, LINE):
        pl.semaphore_signal(
            barrier, inc=1, device_id={"seq": lax.rem(z + i, LINE) * LINE + r}, device_id_type=MESH
        )
        pl.semaphore_signal(
            barrier, inc=1, device_id={"seq": z * LINE + lax.rem(r + i, LINE)}, device_id_type=MESH
        )

    pltpu.make_async_copy(label_ref.at[z], zlab.at[z], l_recv.at[z]).start()
    for a in range(4):
        pltpu.make_async_copy(
            sources[a].at[:, lanes(z)], zbuf.at[z, a], z_recv.at[z, a]
        ).start()

    before = mask(
        lax.broadcasted_iota(jnp.int32, (ROWS, ROWS), 0)
        < lax.broadcasted_iota(jnp.int32, (ROWS, ROWS), 1)
    )

    def prepare(s):
        wait_for(zlab.at[s], l_recv.at[s])
        label = zlab[s]
        named = (
            lax.broadcasted_iota(jnp.int32, (CLUSTERS, ROWS), 0) == label
        ).astype(F32)
        rank = jnp.sum(named * dot(named.astype(BF16), before), axis=0, keepdims=True)
        slot = label * MOST + rank.astype(jnp.int32)
        pick[s] = mask(lax.broadcasted_iota(jnp.int32, (SLOTS, ROWS), 0) == slot)
        column = jnp.broadcast_to(slot.astype(F32), (DIM, ROWS)).T[:, 0:1].astype(jnp.int32)
        back[s] = mask(lax.broadcasted_iota(jnp.int32, (ROWS, SLOTS), 1) == column)

    prepare(z)
    pl.semaphore_wait(barrier, 2 * (LINE - 1))

    def send_z(n, _):
        dist, at = inward(n)
        to = (z + dist) % LINE
        for a in range(4):
            @pl.when(at == a)
            def _():
                pltpu.make_async_remote_copy(
                    src_ref=sources[a].at[:, lanes(to)], dst_ref=zbuf.at[z, a],
                    send_sem=z_send.at[dist], recv_sem=z_recv.at[z, a],
                    device_id={"seq": to * LINE + r}, device_id_type=MESH,
                ).start()
        return 0

    def send_label(i, _):
        to = (z + i) % LINE
        pltpu.make_async_remote_copy(
            src_ref=label_ref.at[to], dst_ref=zlab.at[z], send_sem=l_send, recv_sem=l_recv.at[z],
            device_id={"seq": to * LINE + r}, device_id_type=MESH,
        ).start()
        return 0

    lax.fori_loop(1, LINE, send_label, 0)
    lax.fori_loop(4, 4 + WINDOW, send_z, 0)

    def to_owners(s, a, buf, send_sem, recv_sem):
        pltpu.make_async_copy(
            xsrc.at[s, a, piece(r)], buf.at[s, a, piece(r)], recv_sem.at[s, a]
        ).start()

        def send(n, _):
            o = (r + n) % LINE
            pltpu.make_async_remote_copy(
                src_ref=xsrc.at[s, a, piece(o)], dst_ref=buf.at[s, a, piece(r)],
                send_sem=send_sem.at[s, a], recv_sem=recv_sem.at[s, a],
                device_id={"seq": z * LINE + o}, device_id_type=MESH,
            ).start()
            return 0

        lax.fori_loop(1, LINE, send, 0)

    def pack(n, _):
        dist, a = inward(n)
        s = (z - dist + LINE) % LINE

        @pl.when((a == 0) & (n > 0))
        def _():
            prepare(s)

        wait_for(zbuf.at[s, a], z_recv.at[s, a])
        xsrc[s, a] = dot(pick[s], zbuf[s, a]).astype(BF16)

        @pl.when(a == 1)
        def _():
            used = jnp.sum(pick[s].astype(F32), axis=1, keepdims=True)
            first = lax.broadcasted_iota(jnp.int32, (SLOTS, DIM), 1) == 0
            mark = jnp.where(first, (1.0 - used) * ABSENT, 0.0)
            xsrc[s, 1] = (xsrc[s, 1].astype(F32) + mark).astype(BF16)

        to_owners(s, a, xbuf, x_send, x_recv)

        @pl.when((n + WINDOW >= 4 + WINDOW) & (n + WINDOW < 32))
        def _():
            send_z(n + WINDOW, 0)

        return 0

    def regroup(n, _):
        dist, a = inward(n)
        s = (z - dist + LINE) % LINE
        wait_for(xbuf.at[s, a], x_recv.at[s, a])
        for half in range(2):
            moved = dot(
                order_ref[...], xbuf[s, a, half * HALF:(half + 1) * HALF]
            ).astype(BF16)
            for j in range(OWNED):
                at = pl.multiple_of(s * PIECE + half * RUN, 16)
                x[j, a, pl.ds(at, RUN), :] = moved[j * RUN:(j + 1) * RUN]
        return 0

    def arrive(n, _):
        pack(n, 0)
        lo = jnp.where(n < 14, jnp.maximum(n - 7, 0), 7 + (3 * (n - 14) + 1) // 2)
        hi = jnp.where(n < 14, jnp.maximum(n - 6, 0), lo + 2 - n % 2)
        lax.fori_loop(lo, hi, regroup, 0)
        return 0

    def spread(n, _):
        dist, a = outward(n)
        s = (z + dist) % LINE
        wait_for(xsrc.at[s, a, pl.ds(0, SLOTS - PIECE)], x_send.at[s, a])
        for half in range(2):
            at = pl.multiple_of(s * PIECE + half * RUN, 16)
            rows = jnp.concatenate([y[j, a, pl.ds(at, RUN), :] for j in range(OWNED)], axis=0)
            xsrc[s, a, half * HALF:(half + 1) * HALF] = dot(undo_ref[...], rows).astype(BF16)
        to_owners(s, a, ybuf, y_send, y_recv)
        return 0

    def deliver(n, _):
        dist, at = outward(n)
        s = (z + dist) % LINE
        wait_for(ybuf.at[s, at], y_recv.at[s, at])
        zbuf[s, at] = dot(back[s], ybuf[s, at]).astype(BF16)
        for a in range(4):
            @pl.when((at == a) & (s != z))
            def _():
                pltpu.make_async_remote_copy(
                    src_ref=zbuf.at[s, a], dst_ref=results[a].at[:, lanes(z)],
                    send_sem=o_send.at[s], recv_sem=o_recv.at[z],
                    device_id={"seq": s * LINE + r}, device_id_type=MESH,
                ).start()

            @pl.when((at == a) & (s == z))
            def _():
                pltpu.make_async_copy(
                    zbuf.at[z, a], results[a].at[:, lanes(z)], o_recv.at[z]
                ).start()
        return 0

    lax.fori_loop(0, 18, arrive, 0)
    lax.fori_loop(18, 20, pack, 0)
    lax.fori_loop(13, 18, regroup, 0)
    lax.fori_loop(20, 22, pack, 0)

    def score(i, _):
        softmax(x, weights, top, inv, 2 * i)
        softmax(x, weights, top, inv, 2 * i + 1)
        lo = jnp.where(i < 3, 22, 24)
        hi = jnp.where(i < 2, 22, jnp.where(i < 3, 24, 25))
        lax.fori_loop(lo, hi, pack, 0)
        regroup(18 + i, 0)
        return 0

    lax.fori_loop(0, 4, score, 0)
    lax.fori_loop(25, 27, pack, 0)
    lax.fori_loop(22, 25, regroup, 0)

    def attend_one(j, _):
        attend(x, y, weights, j)
        return 0

    lax.fori_loop(0, OWNED, attend_one, 0)
    lax.fori_loop(0, 3, spread, 0)
    lax.fori_loop(27, 29, pack, 0)
    deliver(0, 0)
    lax.fori_loop(25, 27, regroup, 0)
    deliver(1, 0)
    lax.fori_loop(29, 31, pack, 0)
    deliver(2, 0)
    pack(31, 0)
    lax.fori_loop(3, 5, spread, 0)
    lax.fori_loop(27, 32, regroup, 0)

    def value_one(j, _):
        value_gradient(x, y, weights, j)

        @pl.when(j < 3)
        def _():
            spread(j + 5, 0)

        @pl.when(j % 4 == 3)
        def _():
            deliver(3 + j // 4, 0)

        return 0

    lax.fori_loop(0, OWNED, value_one, 0)
    lax.fori_loop(8, 10, spread, 0)

    def behind(i, _):
        backward(x, y, top, inv, dk_acc, i)
        deliver(i + 5, 0)

        @pl.when(i < 6)
        def _():
            spread(i + 10, 0)

        return 0

    lax.fori_loop(0, OWNED, behind, 0)
    lax.fori_loop(16, 13 + AHEAD, spread, 0)

    def leave(n, _):
        @pl.when(n + AHEAD < 32)
        def _():
            spread(n + AHEAD, 0)

        deliver(n, 0)
        return 0

    lax.fori_loop(13, 32, leave, 0)

    def drain(i, _):
        wait_for(zbuf.at[i], o_recv.at[i])
        for a in range(4):
            wait_for(xsrc.at[i, a, pl.ds(0, SLOTS - PIECE)], y_send.at[i, a])

        @pl.when(i != z)
        def _():
            wait_for(zbuf.at[i], o_send.at[i])

        @pl.when(i > 0)
        def _():
            wait_for(zbuf.at[i], z_send.at[i])
            wait_for(zlab.at[i], l_send)

        return 0

    lax.fori_loop(0, LINE, drain, 0)


def regroup_order():
    to = np.arange(HALF)
    source = (to % RUN) // MOST * PIECE + to // RUN * MOST + to % MOST
    return (to[None, :] == source[:, None]).astype(np.float32)


def finish_kernel(*refs):
    held, came, went = refs[8:]
    ins = [pltpu.make_async_copy(refs[a], held.at[a], came.at[a]) for a in range(4)]
    outs = [pltpu.make_async_copy(held.at[a], refs[4 + a], went.at[a]) for a in range(4)]
    for a in range(4):
        ins[a].start()
    for a in range(4):
        ins[a].wait()
        outs[a].start()
    for a in range(4):
        outs[a].wait()


def per_device(queries, keys, values, grad_out, cluster):
    dma = pltpu.SemaphoreType.DMA
    labels = cluster.reshape(HEADS, 1, ROWS)
    order = regroup_order()
    outs = pl.pallas_call(
        kernel,
        out_shape=[jax.ShapeDtypeStruct((ROWS, HEADS * DIM), BF16)] * 4,
        in_specs=[pl.BlockSpec(memory_space=ANY)] * 4 + [pl.BlockSpec(memory_space=VMEM)] * 3,
        out_specs=[pl.BlockSpec(memory_space=ANY)] * 4,
        scratch_shapes=[
            VMEM((LINE, 4, ROWS, DIM), BF16),
            VMEM((LINE, 1, ROWS), jnp.int32),
            VMEM((LINE, SLOTS, ROWS), BF16),
            VMEM((LINE, ROWS, SLOTS), BF16),
            VMEM((LINE, 4, SLOTS, DIM), BF16),
            VMEM((LINE, 4, SLOTS, DIM), BF16),
            VMEM((LINE, 4, SLOTS, DIM), BF16),
            VMEM((OWNED, 4, CAP, DIM), BF16),
            VMEM((OWNED, 4, CAP, DIM), BF16),
            VMEM((OWNED, 3 * BLOCK_FWD, BLOCK_FWD), BF16),
            VMEM((OWNED, 1, CAP), F32),
            VMEM((OWNED, 1, CAP), F32),
            VMEM((CAP, DIM), F32),
            dma((LINE,)), dma((LINE, 4)), dma, dma((LINE,)),
            dma((LINE, 4)), dma((LINE, 4)), dma((LINE, 4)), dma((LINE, 4)),
            dma((LINE,)), dma((LINE,)),
        ],
        compiler_params=pltpu.CompilerParams(
            collective_id=0, has_side_effects=True, vmem_limit_bytes=60 * 2**20
        ),
        name="attention",
    )(queries, keys, values, grad_out, labels, jnp.asarray(order, BF16), jnp.asarray(order.T, BF16))
    return pl.pallas_call(
        finish_kernel,
        out_shape=[jax.ShapeDtypeStruct((ROWS, HEADS * DIM), BF16)] * 4,
        in_specs=[pl.BlockSpec(memory_space=ANY)] * 4,
        out_specs=[pl.BlockSpec(memory_space=ANY)] * 4,
        scratch_shapes=[VMEM((4, ROWS, HEADS * DIM), BF16), dma((4,)), dma((4,))],
        compiler_params=pltpu.CompilerParams(vmem_limit_bytes=60 * 2**20),
        name="finish",
    )(*outs)


def solution(mesh):
    return jax.shard_map(
        per_device,
        mesh=mesh,
        in_specs=(
            P(("grp", "seq"), None),
            P(("grp", "seq"), None),
            P(("grp", "seq"), None),
            P(("grp", "seq"), None),
            P(None, ("grp", "seq"), None),
        ),
        out_specs=(P(("grp", "seq"), None),) * 4,
        check_vma=False,
    )
```

```python
import jax
import jax.numpy as jnp
import numpy as np
from jax import lax
from jax.experimental import pallas as pl
from jax.experimental.pallas import tpu as pltpu
from jax.sharding import PartitionSpec as P

MESH = pl.DeviceIdType.MESH
HEADS = 8
DIM = 128
ROWS = 384
CLUSTERS = 64
MOST = 12
LINE = 8
OWNED = 8
PIECE = OWNED * MOST
SLOTS = LINE * PIECE
CAP = LINE * LINE * MOST
HALF = SLOTS // 2
RUN = HALF // OWNED
WINDOW = 6
AHEAD = 6
ABSENT = 64.0
NEG = -1e30
SCALE = DIM ** -0.5
LOG2E = 1.4426950408889634
BLOCK_FWD = 384
BLOCK_BWD = 256
F32, BF16 = jnp.float32, jnp.bfloat16
NT = (((1,), (1,)), ((), ()))
VMEM = pltpu.VMEM
ANY = pl.ANY


def inward(n):
    m = n - 4
    pair, late = m // 4 + 1, (n - 18) % 7
    signed = jnp.where(m % 2 == 0, pair, LINE - pair)
    alone = jnp.where(
        late == 6, 4, jnp.where(late % 2 == 0, late // 2 + 1, LINE - 1 - late // 2)
    )
    dist = jnp.where(
        n < 4, 0, jnp.where(n < 16, signed, jnp.where(n < 18, 4, alone))
    )
    a = jnp.where(
        n < 4, n, jnp.where(n < 16, m % 4 // 2, jnp.where(n < 18, n - 16, jnp.where(n < 25, 2, 3)))
    )
    return dist, a


def outward(n):
    i, m = n % LINE, n - 18
    pair = 3 - m // 4
    alone = jnp.where(i % 2 == 1, 4 - (i + 1) // 2, 4 + i // 2)
    signed = jnp.where(m % 2 == 0, pair, LINE - pair)
    dist = jnp.where(
        n < 16, alone, jnp.where(n < 18, 4, jnp.where(n < 30, signed, 0))
    )
    a = jnp.where(
        n < 8, 0,
        jnp.where(n < 16, 3, jnp.where(n < 18, n - 15, jnp.where(n < 30, m % 4 // 2 + 1, n - 29))),
    )
    return dist, a


def wait_for(ref, sem):
    pltpu.make_async_copy(ref, ref, sem).wait()


def piece(o):
    return pl.ds(pl.multiple_of(o * PIECE, PIECE), PIECE)


def lanes(h):
    return pl.ds(pl.multiple_of(h * DIM, DIM), DIM)


def dot(a, b):
    return jnp.dot(a, b, preferred_element_type=F32)


def dot_nt(a, b):
    return lax.dot_general(a, b, NT, preferred_element_type=F32)


def mask(m):
    return m.astype(F32).astype(BF16)


def scores(k, q, bias, lo, hi):
    t = dot_nt(k[:hi], q) * (SCALE * LOG2E) + bias[:hi]
    late = (
        lax.broadcasted_iota(jnp.int32, (hi - lo, hi - lo), 0)
        > lax.broadcasted_iota(jnp.int32, (hi - lo, hi - lo), 1)
    )
    own = jnp.where(late, NEG, t[lo:hi])
    return jnp.concatenate([t[:lo], own], axis=0) if lo else own


def softmax(x, weights, top_ref, inv_ref, j):
    k = x[j, 1]
    bias = jnp.where(k[:, 0:1].astype(F32) > ABSENT / 2, NEG, 0.0)
    at = 0
    for lo in range(0, CAP, BLOCK_FWD):
        hi = lo + BLOCK_FWD
        t = scores(k, x[j, 0, lo:hi], bias, lo, hi)
        top = jnp.max(t, axis=0, keepdims=True)
        powered = jnp.exp2(t - top)
        inv = 1.0 / jnp.sum(powered, axis=0, keepdims=True)
        top_ref[j, :, lo:hi] = top
        inv_ref[j, :, lo:hi] = inv
        weights[j, at:at + hi] = (powered * inv).astype(BF16)
        at += hi


def attend(x, y, weights, j):
    vt = x[j, 2].T
    at = 0
    for hi in range(BLOCK_FWD, CAP + 1, BLOCK_FWD):
        y[j, 0, hi - BLOCK_FWD:hi] = dot(vt[:, :hi], weights[j, at:at + hi]).T.astype(BF16)
        at += hi


def value_gradient(x, y, weights, j):
    g = x[j, 3]
    half = BLOCK_FWD
    y[j, 3, :half] = (
        dot(weights[j, :half], g[:half]) + dot(weights[j, half:2 * half], g[half:])
    ).astype(BF16)
    y[j, 3, half:] = dot(weights[j, 2 * half:], g[half:]).astype(BF16)


def backward(x, y, top_ref, inv_ref, dk_acc, j):
    k, v = x[j, 1], x[j, 2]
    kt = k.T
    bias = jnp.where(k[:, 0:1].astype(F32) > ABSENT / 2, NEG, 0.0)
    for lo in range(0, CAP, BLOCK_BWD):
        hi = lo + BLOCK_BWD
        q, g = x[j, 0, lo:hi], x[j, 3, lo:hi]
        t = scores(k, q, bias, lo, hi)
        weights = jnp.exp2(t - top_ref[j, :, lo:hi]) * inv_ref[j, :, lo:hi]
        row_dot = jnp.sum(
            (g.astype(F32) * y[j, 0, lo:hi].astype(F32)).T, axis=0, keepdims=True
        )
        ds = (weights * (dot_nt(v[:hi], g) - row_dot)).astype(BF16)
        dk = dot(ds, q)
        y[j, 1, lo:hi] = (dot(kt[:, :hi], ds) * SCALE).T.astype(BF16)
        if lo:
            dk_acc[:lo] += dk[:lo]
        dk_acc[lo:hi] = dk[lo:]
    y[j, 2] = (dk_acc[...] * SCALE).astype(BF16)


def kernel(
    q_ref, k_ref, v_ref, g_ref, label_ref, order_ref, undo_ref,
    o_ref, dq_ref, dk_ref, dv_ref,
    zbuf, zlab, pick, back, xsrc, xbuf, ybuf, x, y, weights, top, inv, dk_acc,
    z_send, z_recv, l_send, l_recv, x_send, x_recv, y_send, y_recv, o_send, o_recv,
):
    me = lax.axis_index("seq")
    z, r = me // LINE, me % LINE
    sources = (q_ref, k_ref, v_ref, g_ref)
    results = (o_ref, dq_ref, dk_ref, dv_ref)

    barrier = pltpu.get_barrier_semaphore()
    for i in range(1, LINE):
        pl.semaphore_signal(
            barrier, inc=1, device_id={"seq": lax.rem(z + i, LINE) * LINE + r}, device_id_type=MESH
        )
        pl.semaphore_signal(
            barrier, inc=1, device_id={"seq": z * LINE + lax.rem(r + i, LINE)}, device_id_type=MESH
        )

    pltpu.make_async_copy(label_ref.at[z], zlab.at[z], l_recv.at[z]).start()
    for a in range(4):
        pltpu.make_async_copy(
            sources[a].at[:, lanes(z)], zbuf.at[z, a], z_recv.at[z, a]
        ).start()

    before = mask(
        lax.broadcasted_iota(jnp.int32, (ROWS, ROWS), 0)
        < lax.broadcasted_iota(jnp.int32, (ROWS, ROWS), 1)
    )

    def prepare(s):
        wait_for(zlab.at[s], l_recv.at[s])
        label = zlab[s]
        named = (
            lax.broadcasted_iota(jnp.int32, (CLUSTERS, ROWS), 0) == label
        ).astype(F32)
        rank = jnp.sum(named * dot(named.astype(BF16), before), axis=0, keepdims=True)
        slot = label * MOST + rank.astype(jnp.int32)
        pick[s] = mask(lax.broadcasted_iota(jnp.int32, (SLOTS, ROWS), 0) == slot)
        column = jnp.broadcast_to(slot.astype(F32), (DIM, ROWS)).T[:, 0:1].astype(jnp.int32)
        back[s] = mask(lax.broadcasted_iota(jnp.int32, (ROWS, SLOTS), 1) == column)

    prepare(z)
    pl.semaphore_wait(barrier, 2 * (LINE - 1))

    def send_z(n, _):
        dist, at = inward(n)
        to = (z + dist) % LINE
        for a in range(4):
            @pl.when(at == a)
            def _():
                pltpu.make_async_remote_copy(
                    src_ref=sources[a].at[:, lanes(to)], dst_ref=zbuf.at[z, a],
                    send_sem=z_send.at[dist], recv_sem=z_recv.at[z, a],
                    device_id={"seq": to * LINE + r}, device_id_type=MESH,
                ).start()
        return 0

    def send_label(i, _):
        to = (z + i) % LINE
        pltpu.make_async_remote_copy(
            src_ref=label_ref.at[to], dst_ref=zlab.at[z], send_sem=l_send, recv_sem=l_recv.at[z],
            device_id={"seq": to * LINE + r}, device_id_type=MESH,
        ).start()
        return 0

    lax.fori_loop(1, LINE, send_label, 0)
    lax.fori_loop(4, 4 + WINDOW, send_z, 0)

    def to_owners(s, a, buf, send_sem, recv_sem):
        pltpu.make_async_copy(
            xsrc.at[s, a, piece(r)], buf.at[s, a, piece(r)], recv_sem.at[s, a]
        ).start()

        def send(n, _):
            o = (r + n) % LINE
            pltpu.make_async_remote_copy(
                src_ref=xsrc.at[s, a, piece(o)], dst_ref=buf.at[s, a, piece(r)],
                send_sem=send_sem.at[s, a], recv_sem=recv_sem.at[s, a],
                device_id={"seq": z * LINE + o}, device_id_type=MESH,
            ).start()
            return 0

        lax.fori_loop(1, LINE, send, 0)

    def pack(n, _):
        dist, a = inward(n)
        s = (z - dist + LINE) % LINE

        @pl.when((a == 0) & (n > 0))
        def _():
            prepare(s)

        wait_for(zbuf.at[s, a], z_recv.at[s, a])
        xsrc[s, a] = dot(pick[s], zbuf[s, a]).astype(BF16)

        @pl.when(a == 1)
        def _():
            used = jnp.sum(pick[s].astype(F32), axis=1, keepdims=True)
            first = lax.broadcasted_iota(jnp.int32, (SLOTS, DIM), 1) == 0
            mark = jnp.where(first, (1.0 - used) * ABSENT, 0.0)
            xsrc[s, 1] = (xsrc[s, 1].astype(F32) + mark).astype(BF16)

        to_owners(s, a, xbuf, x_send, x_recv)

        @pl.when((n + WINDOW >= 4 + WINDOW) & (n + WINDOW < 32))
        def _():
            send_z(n + WINDOW, 0)

        return 0

    def regroup(n, _):
        dist, a = inward(n)
        s = (z - dist + LINE) % LINE
        wait_for(xbuf.at[s, a], x_recv.at[s, a])
        for half in range(2):
            moved = dot(
                order_ref[...], xbuf[s, a, half * HALF:(half + 1) * HALF]
            ).astype(BF16)
            for j in range(OWNED):
                at = pl.multiple_of(s * PIECE + half * RUN, 16)
                x[j, a, pl.ds(at, RUN), :] = moved[j * RUN:(j + 1) * RUN]
        return 0

    def arrive(n, _):
        pack(n, 0)
        lo = jnp.where(n < 14, jnp.maximum(n - 7, 0), 7 + (3 * (n - 14) + 1) // 2)
        hi = jnp.where(n < 14, jnp.maximum(n - 6, 0), lo + 2 - n % 2)
        lax.fori_loop(lo, hi, regroup, 0)
        return 0

    def spread(n, _):
        dist, a = outward(n)
        s = (z + dist) % LINE
        wait_for(xsrc.at[s, a, pl.ds(0, SLOTS - PIECE)], x_send.at[s, a])
        for half in range(2):
            at = pl.multiple_of(s * PIECE + half * RUN, 16)
            rows = jnp.concatenate([y[j, a, pl.ds(at, RUN), :] for j in range(OWNED)], axis=0)
            xsrc[s, a, half * HALF:(half + 1) * HALF] = dot(undo_ref[...], rows).astype(BF16)
        to_owners(s, a, ybuf, y_send, y_recv)
        return 0

    def deliver(n, _):
        dist, at = outward(n)
        s = (z + dist) % LINE
        wait_for(ybuf.at[s, at], y_recv.at[s, at])
        zbuf[s, at] = dot(back[s], ybuf[s, at]).astype(BF16)
        for a in range(4):
            @pl.when((at == a) & (s != z))
            def _():
                pltpu.make_async_remote_copy(
                    src_ref=zbuf.at[s, a], dst_ref=results[a].at[:, lanes(z)],
                    send_sem=o_send.at[s], recv_sem=o_recv.at[z],
                    device_id={"seq": s * LINE + r}, device_id_type=MESH,
                ).start()

            @pl.when((at == a) & (s == z))
            def _():
                pltpu.make_async_copy(
                    zbuf.at[z, a], results[a].at[:, lanes(z)], o_recv.at[z]
                ).start()
        return 0

    lax.fori_loop(0, 18, arrive, 0)
    lax.fori_loop(18, 20, pack, 0)
    lax.fori_loop(13, 18, regroup, 0)
    lax.fori_loop(20, 22, pack, 0)

    def score(i, _):
        softmax(x, weights, top, inv, 2 * i)
        softmax(x, weights, top, inv, 2 * i + 1)
        lo = jnp.where(i < 3, 22, 24)
        hi = jnp.where(i < 2, 22, jnp.where(i < 3, 24, 25))
        lax.fori_loop(lo, hi, pack, 0)
        regroup(18 + i, 0)
        return 0

    lax.fori_loop(0, 4, score, 0)
    lax.fori_loop(25, 27, pack, 0)
    lax.fori_loop(22, 25, regroup, 0)

    def attend_one(j, _):
        attend(x, y, weights, j)
        return 0

    lax.fori_loop(0, OWNED, attend_one, 0)
    lax.fori_loop(27, 29, pack, 0)
    lax.fori_loop(0, 2, spread, 0)
    lax.fori_loop(29, 31, pack, 0)
    deliver(0, 0)
    lax.fori_loop(25, 27, regroup, 0)
    pack(31, 0)
    lax.fori_loop(2, 5, spread, 0)
    deliver(1, 0)
    lax.fori_loop(27, 32, regroup, 0)

    def value_one(j, _):
        value_gradient(x, y, weights, j)

        @pl.when(j < 3)
        def _():
            spread(j + 5, 0)

        @pl.when(j % 4 == 3)
        def _():
            deliver(2 + j // 4, 0)

        return 0

    lax.fori_loop(0, OWNED, value_one, 0)
    lax.fori_loop(8, 10, spread, 0)

    def behind(i, _):
        backward(x, y, top, inv, dk_acc, i)
        deliver(i + 4, 0)

        @pl.when(i < 6)
        def _():
            spread(i + 10, 0)

        return 0

    lax.fori_loop(0, OWNED, behind, 0)
    lax.fori_loop(16, 12 + AHEAD, spread, 0)

    def leave(n, _):
        @pl.when(n + AHEAD < 32)
        def _():
            spread(n + AHEAD, 0)

        deliver(n, 0)
        return 0

    lax.fori_loop(12, 32, leave, 0)

    def drain(i, _):
        wait_for(zbuf.at[i], o_recv.at[i])
        for a in range(4):
            wait_for(xsrc.at[i, a, pl.ds(0, SLOTS - PIECE)], y_send.at[i, a])

        @pl.when(i != z)
        def _():
            wait_for(zbuf.at[i], o_send.at[i])

        @pl.when(i > 0)
        def _():
            wait_for(zbuf.at[i], z_send.at[i])
            wait_for(zlab.at[i], l_send)

        return 0

    lax.fori_loop(0, LINE, drain, 0)


def regroup_order():
    to = np.arange(HALF)
    source = (to % RUN) // MOST * PIECE + to // RUN * MOST + to % MOST
    return (to[None, :] == source[:, None]).astype(np.float32)


def finish_kernel(*refs):
    held, came, went = refs[8:]
    ins = [pltpu.make_async_copy(refs[a], held.at[a], came.at[a]) for a in range(4)]
    outs = [pltpu.make_async_copy(held.at[a], refs[4 + a], went.at[a]) for a in range(4)]
    for a in range(4):
        ins[a].start()
    for a in range(4):
        ins[a].wait()
        outs[a].start()
    for a in range(4):
        outs[a].wait()


def per_device(queries, keys, values, grad_out, cluster):
    dma = pltpu.SemaphoreType.DMA
    labels = cluster.reshape(HEADS, 1, ROWS)
    order = regroup_order()
    outs = pl.pallas_call(
        kernel,
        out_shape=[jax.ShapeDtypeStruct((ROWS, HEADS * DIM), BF16)] * 4,
        in_specs=[pl.BlockSpec(memory_space=ANY)] * 4 + [pl.BlockSpec(memory_space=VMEM)] * 3,
        out_specs=[pl.BlockSpec(memory_space=ANY)] * 4,
        scratch_shapes=[
            VMEM((LINE, 4, ROWS, DIM), BF16),
            VMEM((LINE, 1, ROWS), jnp.int32),
            VMEM((LINE, SLOTS, ROWS), BF16),
            VMEM((LINE, ROWS, SLOTS), BF16),
            VMEM((LINE, 4, SLOTS, DIM), BF16),
            VMEM((LINE, 4, SLOTS, DIM), BF16),
            VMEM((LINE, 4, SLOTS, DIM), BF16),
            VMEM((OWNED, 4, CAP, DIM), BF16),
            VMEM((OWNED, 4, CAP, DIM), BF16),
            VMEM((OWNED, 3 * BLOCK_FWD, BLOCK_FWD), BF16),
            VMEM((OWNED, 1, CAP), F32),
            VMEM((OWNED, 1, CAP), F32),
            VMEM((CAP, DIM), F32),
            dma((LINE,)), dma((LINE, 4)), dma, dma((LINE,)),
            dma((LINE, 4)), dma((LINE, 4)), dma((LINE, 4)), dma((LINE, 4)),
            dma((LINE,)), dma((LINE,)),
        ],
        compiler_params=pltpu.CompilerParams(
            collective_id=0, has_side_effects=True, vmem_limit_bytes=60 * 2**20
        ),
        name="attention",
    )(queries, keys, values, grad_out, labels, jnp.asarray(order, BF16), jnp.asarray(order.T, BF16))
    return pl.pallas_call(
        finish_kernel,
        out_shape=[jax.ShapeDtypeStruct((ROWS, HEADS * DIM), BF16)] * 4,
        in_specs=[pl.BlockSpec(memory_space=ANY)] * 4,
        out_specs=[pl.BlockSpec(memory_space=ANY)] * 4,
        scratch_shapes=[VMEM((4, ROWS, HEADS * DIM), BF16), dma((4,)), dma((4,))],
        compiler_params=pltpu.CompilerParams(vmem_limit_bytes=60 * 2**20),
        name="finish",
    )(*outs)


def solution(mesh):
    return jax.shard_map(
        per_device,
        mesh=mesh,
        in_specs=(
            P(("grp", "seq"), None),
            P(("grp", "seq"), None),
            P(("grp", "seq"), None),
            P(("grp", "seq"), None),
            P(None, ("grp", "seq"), None),
        ),
        out_specs=(P(("grp", "seq"), None),) * 4,
        check_vma=False,
    )
```
